256 devices in a mesh: dp: 8 (over z), space: 32 (over y, x, core).
Axes of the slice: x: 4, y: 4, z: 8, core: 2. Of those that a mesh axis runs over, the one named last changes fastest.
Arguments:
- fields: bfloat16 [8, 64, 64, 4096], P('dp', 'space'), may hold values from -6 to 6
- spec_weights: bfloat16 [32, 1024, 64, 128], P(None, ('dp', 'space')), may hold values from -0.75 to 0.75
- local_weight: bfloat16 [64, 64], replicated, may hold values from -0.75 to 0.75
- bias: float32 [64], replicated, may hold values from -3 to 3
- cotangent: bfloat16 [8, 64, 64, 4096], P('dp', 'space'), may hold values from -6 to 6
Outputs:
- output: bfloat16 [8, 64, 64, 4096], P('dp', 'space')
- grad_input: bfloat16 [8, 64, 64, 4096], P('dp', 'space')
- grad_weights: float32 [32, 1024, 64, 128], P(None, ('dp', 'space'))
The draws below stay inside these ranges and needn't reach their ends.
All inputs are finite; a program needn't handle non-finite values.
Results may differ from the reference program's by a relative error of at most 0.015.
Values may be sent and summed in bfloat16 or wider, within the bound.
A program may use at most 128 MiB of HBM per device.

```python
import math
from functools import partial
import jax
import jax.numpy as jnp

GRID = 64
CH = 64
MODES = 32
SAMPLES = 8


def shard_levels(stream_key, shape, shards, smallest, top_value):
    level = 1.0
    for position, blocks in shards:
        heights = jax.random.uniform(jax.random.fold_in(jax.random.fold_in(stream_key, 6), position), (blocks,), jnp.float32, smallest / len(shards), top_value / len(shards))
        level = level * jnp.repeat(jnp.exp(heights), shape[position] // blocks).reshape((-1,) + (1,) * (len(shape) - 1 - position))
    return level


def noise(rng, shape, scale, most, split=(), held_as=jnp.bfloat16):
    level = shard_levels(rng, shape, split, -0.22, 0.18) if split else 1.0
    values = jax.random.normal(rng, shape, jnp.float32) * scale * level
    return jnp.minimum(jnp.maximum(values, -most), most).astype(held_as)


def setup_inputs(seed: int = 0) -> dict:
    seeds = jax.random.split(jax.random.key(seed), 6)
    fields = noise(seeds[0], (SAMPLES, GRID, CH, GRID * GRID), 1.0, 6.0, ((0, 8), (1, 32)))
    spec_weights = noise(seeds[1], (MODES, MODES * MODES, CH, 2 * CH), CH ** -0.5, 0.75, ((1, 256),))
    local_weight = noise(seeds[2], (CH, CH), CH ** -0.5, 0.75)
    bias = noise(seeds[3], (CH,), 0.5, 3.0, (), jnp.float32)
    cotangent = noise(seeds[4], (SAMPLES, GRID, CH, GRID * GRID), 1.0, 6.0, ((0, 8), (1, 32)))
    return {"fields": fields, "spec_weights": spec_weights, "local_weight": local_weight, "bias": bias, "cotangent": cotangent}


def make_tables(grid_size, mode_count):
    half_count = mode_count // 2
    mode_index = jnp.arange(mode_count, dtype=jnp.int32)
    signed = jnp.where(mode_index < half_count, mode_index, grid_size - mode_count + mode_index).astype(jnp.int32)
    cell_index = jnp.arange(grid_size, dtype=jnp.int32)
    freq_y = jnp.repeat(signed, mode_count)
    freq_z = jnp.tile(mode_index, mode_count)
    cell_y = jnp.repeat(cell_index, grid_size)
    cell_z = jnp.tile(cell_index, grid_size)
    phases = (cell_y[:, None] * freq_y[None, :] + cell_z[:, None] * freq_z[None, :]) % grid_size
    angles = phases.astype(jnp.float32) * (2.0 * math.pi / grid_size)
    yz_table = (jnp.stack([jnp.cos(angles), -jnp.sin(angles)], axis=1) / grid_size).astype(jnp.bfloat16)
    phase_x = signed[:, None] * cell_index[None, :] % grid_size
    angle_x = phase_x.astype(jnp.float32) * (2.0 * math.pi / grid_size)
    cosine = jnp.cos(angle_x) / math.sqrt(grid_size)
    sine_x = jnp.sin(angle_x) / math.sqrt(grid_size)
    forward_x = jnp.stack([jnp.stack([cosine, sine_x]), jnp.stack([-sine_x, cosine])]).astype(jnp.bfloat16)
    inverse_x = jnp.stack([jnp.stack([cosine.T, -sine_x.T]), jnp.stack([sine_x.T, cosine.T])]).astype(jnp.bfloat16)
    halves = jnp.where(freq_z == 0, 1.0, 2.0).astype(jnp.bfloat16)
    return (yz_table, forward_x, inverse_x, halves)

def yz_forward(values, yz_table):
    result = jnp.einsum('bxcn,nrp->bxprc', values.astype(jnp.float32), yz_table.astype(jnp.float32))
    return result.reshape(result.shape[0], result.shape[1], result.shape[2], 2 * result.shape[4])

def yz_inverse(values, yz_table):
    paired = values.reshape(values.shape[0], values.shape[1], values.shape[2], 2, values.shape[3] // 2)
    return jnp.einsum('bxprc,nrp->bxcn', paired.astype(jnp.float32), yz_table.astype(jnp.float32))

def along_x(table, values):
    in_shape = values.shape
    half_width = in_shape[-1] // 2
    middle = tuple(in_shape[2:-1])
    paired = values.reshape(in_shape[0], in_shape[1], -1, 2, half_width)
    result = jnp.einsum('oikx,bxmic->bkmoc', table.astype(jnp.float32), paired.astype(jnp.float32))
    return result.reshape((in_shape[0], table.shape[2]) + middle + (in_shape[-1],))

def rotate_layout(values):
    half_width = values.shape[-1] // 2
    signs = jnp.concatenate([jnp.ones((half_width,), jnp.float32), -jnp.ones((half_width,), jnp.float32)])
    return jnp.roll(values, half_width, axis=-1) * signs.astype(values.dtype)

def spectral_mix_apply(spectrum, weights):
    paired = spectrum.reshape(spectrum.shape[:-1] + (2, spectrum.shape[-1] // 2))
    products = jnp.einsum('skmrc,kmcd->skmrd', paired.astype(jnp.float32), weights.astype(jnp.float32))
    return products[:, :, :, 0] - rotate_layout(products[:, :, :, 1])

def mix_backward(spectrum, grad_mixed, weights):
    stacked = jnp.stack([grad_mixed, rotate_layout(grad_mixed)], axis=3).astype(jnp.float32)
    paired = spectrum.reshape(spectrum.shape[:-1] + (2, spectrum.shape[-1] // 2)).astype(jnp.float32)
    grad_weights = jnp.einsum('skmrc,skmrd->kmcd', paired, stacked)
    grad_spec = jnp.einsum('skmrd,kmcd->skmrc', stacked, weights.astype(jnp.float32))
    return (grad_weights, grad_spec.reshape(spectrum.shape))

def reference(fields, spec_weights, local_weight, bias, cotangent):
    yz_table, forward_x, inverse_x, halves = make_tables(GRID, MODES)
    weighting = halves.astype(jnp.float32)[None, None, :, None]
    grid_spec = yz_forward(fields, yz_table).astype(jnp.bfloat16)
    spectrum = along_x(forward_x, grid_spec).astype(jnp.bfloat16)
    mixed_spec = spectral_mix_apply(spectrum, spec_weights).astype(jnp.bfloat16)
    back_grid = along_x(inverse_x, mixed_spec).astype(jnp.bfloat16)
    spectral = yz_inverse(back_grid.astype(jnp.float32) * weighting, yz_table)
    local_term = jnp.einsum('bxcn,cd->bxdn', fields.astype(jnp.float32), local_weight.astype(jnp.float32))
    preact = spectral + local_term + bias.astype(jnp.float32)[None, None, :, None]
    gelu_exact = partial(jax.nn.gelu, approximate=False)
    output, pullback = jax.vjp(gelu_exact, preact)
    grad_preact = pullback(cotangent.astype(jnp.float32))[0].astype(jnp.bfloat16)
    grad_back = (yz_forward(grad_preact, yz_table) * weighting).astype(jnp.bfloat16)
    grad_mixed = along_x(forward_x, grad_back).astype(jnp.bfloat16)
    grad_weights, grad_spec = mix_backward(spectrum, grad_mixed, spec_weights)
    grad_grid = along_x(inverse_x, grad_spec.astype(jnp.bfloat16)).astype(jnp.bfloat16)
    local_back = jnp.einsum('bxdn,cd->bxcn', grad_preact.astype(jnp.float32), local_weight.astype(jnp.float32))
    grad_input = (yz_inverse(grad_grid, yz_table) + local_back).astype(jnp.bfloat16)
    return (output.astype(jnp.bfloat16), grad_input, grad_weights)
```

```python
import functools
import math

import jax
import jax.numpy as jnp
import ml_dtypes
import numpy as np
from jax import lax
from jax.experimental import pallas as pl
from jax.experimental.pallas import tpu as pltpu
from jax.sharding import PartitionSpec as P

MESH = pl.DeviceIdType.MESH
BF16 = jnp.bfloat16
F32 = jnp.float32

G = 64
M = 32
NS = 32
ND = 8
J = 4
LANES = 128
BLOCKS = 16

NT = (((1,), (1,)), ((), ()))
TN = (((0,), (0,)), ((), ()))


def tables():
    step = 2.0 * math.pi / G
    cell = np.arange(G)
    freq_z = np.arange(M)
    signed = np.where(np.arange(M) < M // 2, np.arange(M), G - M + np.arange(M))
    halves = np.where(freq_z == 0, 1.0, 2.0)
    angle = (freq_z[:, None] * cell[None, :] % G) * step
    z_rows = np.concatenate([np.cos(angle), -np.sin(angle)]) / 8
    z_rows_half = z_rows * np.tile(halves, 2)[:, None]
    four = np.eye(4)
    z_forward = np.kron(four, z_rows)
    z_forward_half = np.kron(four, z_rows_half)
    inv = np.stack([np.cos(angle), -np.sin(angle)], axis=1).reshape(2 * M, G) / 8
    inv_half = inv * np.repeat(halves, 2)[:, None]
    z_inverse = np.kron(four, inv)
    z_inverse_half = np.kron(four, inv_half)
    iy = np.arange(ND)[None, :] * 4 + np.arange(4)[:, None]
    ang_y = (signed[iy][:, :, None] * cell % G) * step
    c, s = np.cos(ang_y) / 8, np.sin(ang_y) / 8
    y_forward = np.stack([np.stack([c, s], -1), np.stack([-s, c], -1)], 1).reshape(64, 128)
    ct, st = c.transpose(2, 0, 1), s.transpose(2, 0, 1)
    y_inverse = np.stack([np.stack([ct, -st], 2), np.stack([st, ct], 2)], 0).reshape(128, 64)
    xs = 2 * np.arange(NS)[None, :] + np.arange(2)[:, None]
    ang_x = (signed[None, :, None] * xs[:, None, :] % G) * step
    c, s = np.cos(ang_x) / 8, np.sin(ang_x) / 8
    x_forward = np.stack([np.stack([c, s], 2), np.stack([-s, c], 2)], 1)
    x_forward = x_forward.reshape(128, 64)
    x_inverse = np.stack([c.transpose(0, 2, 1), s.transpose(0, 2, 1)]).reshape(128, M)
    return [
        t.astype(np.float32).astype(ml_dtypes.bfloat16)
        for t in (
            z_forward, z_forward_half, z_inverse, z_inverse_half,
            y_forward, y_inverse, x_forward, x_inverse,
        )
    ]


def dot(a, b, dims=(((1,), (0,)), ((), ()))):
    return lax.dot_general(a, b, dims, preferred_element_type=F32)


def kernel(
    x_ref, mix_in, mix_back, bias_ref,
    zf, zfh, zi, zih, yf, yi, xf, xi,
    w_hbm, cot_hbm,
    out_hbm, gin_hbm, gw_hbm,
    w_ref, cot_ref, out_ref, gp_ref, gin_ref, gw_ref,
    a_ref, f_ref, v_ref, u_ref, m_ref,
    send_s, recv_s, send_d, recv_d,
    sem_send_s, sem_recv_s, sem_send_d, sem_recv_d, sem_local,
):
    d = lax.axis_index("dp")
    s = lax.axis_index("space")

    w_copy = pltpu.make_async_copy(w_hbm, w_ref, sem_local.at[0])
    w_copy.start()
    cot_copy = pltpu.make_async_copy(cot_hbm, cot_ref, sem_local.at[1])
    cot_copy.start()

    barrier = pltpu.get_barrier_semaphore()

    def greet_space(i, carry):
        pl.semaphore_signal(barrier, inc=1, device_id=(d, lax.rem(s + i, NS)), device_id_type=MESH)
        return carry

    def greet_dp(i, carry):
        pl.semaphore_signal(barrier, inc=1, device_id=(lax.rem(d + i, ND), s), device_id_type=MESH)
        return carry

    lax.fori_loop(1, NS, greet_space, 0)
    lax.fori_loop(1, ND, greet_dp, 0)

    lo = lax.broadcasted_iota(jnp.int32, (1, LANES), 1) < 64

    def swap(v):
        return pltpu.roll(v, 64, 1)

    def exchange_space(n):
        src, dst = send_s.at[n], recv_s.at[n]

        def go(i, carry):
            t = lax.rem(s + i, NS)
            pltpu.make_async_remote_copy(
                src_ref=src.at[t], dst_ref=dst.at[s],
                send_sem=sem_send_s.at[n], recv_sem=sem_recv_s.at[n],
                device_id=(d, t), device_id_type=MESH,
            ).start()
            return carry

        lax.fori_loop(1, NS, go, 0)
        pltpu.make_async_copy(src.at[s], dst.at[s], sem_recv_s.at[n]).start()

    def exchange_dp(n):
        src, dst = send_d.at[n], recv_d.at[n]

        def go(i, carry):
            t = lax.rem(d + i, ND)
            pltpu.make_async_remote_copy(
                src_ref=src.at[t], dst_ref=dst.at[d],
                send_sem=sem_send_d.at[n], recv_sem=sem_recv_d.at[n],
                device_id=(t, s), device_id_type=MESH,
            ).start()
            return carry

        lax.fori_loop(1, ND, go, 0)
        pltpu.make_async_copy(src.at[d], dst.at[d], sem_recv_d.at[n]).start()

    def arrived_space(n):
        pltpu.make_async_copy(recv_s.at[n], recv_s.at[n], sem_recv_s.at[n]).wait()

    def arrived_dp(n):
        pltpu.make_async_copy(recv_d.at[n], recv_d.at[n], sem_recv_d.at[n]).wait()

    def z_forward(block, table, q):
        a_ref[pl.ds(pl.multiple_of(q * 256, 256), 256), :] = dot(table[...], block, NT)

    def y_forward(n):
        def go(izh, carry):
            for pair in range(2):
                parts = [
                    a_ref[pl.ds(izh * 4 + pair * 2 + e, 128, stride=M), :].astype(BF16)
                    for e in range(2)
                ]
                res = dot(yf[...], jnp.concatenate(parts, axis=1)).astype(BF16)
                for e in range(2):
                    for iyl in range(4):
                        send_s[n, iyl * 8 + izh, pair * 2 + e] = res[
                            iyl * 16 : iyl * 16 + 16, e * 128 : e * 128 + 128
                        ]
            return carry

        lax.fori_loop(0, 8, go, 0, unroll=2)

    def x_forward(n_space, n_dp):
        def widen(t, carry):
            f_ref[pl.ds(pl.multiple_of(t * 64, 64), 64), :] = (
                recv_s[n_space, t].reshape(64, LANES).astype(F32)
            )
            return carry

        lax.fori_loop(0, NS, widen, 0, unroll=4)

        def go(dh, carry):
            for pair in range(2):
                parts = []
                for e in range(2):
                    row = (pair * 2 + e) * 16 + dh
                    parts.append(
                        jnp.concatenate(
                            [
                                f_ref[pl.ds(row, NS, stride=64), :],
                                f_ref[pl.ds(row + 8, NS, stride=64), :],
                            ],
                            axis=0,
                        ).astype(BF16)
                    )
                res = dot(xf[...], jnp.concatenate(parts, axis=1))
                for e in range(2):
                    p00, p01, p10, p11 = (
                        res[b * 32 : b * 32 + 32, e * 128 : e * 128 + 128] for b in range(4)
                    )
                    both = jnp.where(lo, p00, p11) + swap(jnp.where(lo, p01, p10))
                    send_d[n_dp, dh, pair * 2 + e] = both.astype(BF16)
            return carry

        lax.fori_loop(0, ND, go, 0, unroll=2)

    def widen_dp(n, to):
        def go(b, carry):
            to[pl.ds(pl.multiple_of(b * 128, 128), 128), :] = (
                recv_d[n, b].reshape(128, LANES).astype(F32)
            )
            return carry

        lax.fori_loop(0, ND, go, 0)

    def narrow_dp(n):
        def go(b, carry):
            send_d[n, b] = (
                m_ref[pl.ds(pl.multiple_of(b * 128, 128), 128), :]
                .astype(BF16)
                .reshape(J, M, LANES)
            )
            return carry

        lax.fori_loop(0, ND, go, 0)

    def x_inverse(n_dp, n_space):
        def go(dh, carry):
            for pair in range(2):
                rhs = jnp.concatenate(
                    [recv_d[n_dp, dh, pair * 2], recv_d[n_dp, dh, pair * 2 + 1]], axis=1
                )
                res = dot(xi[...], rhs)
                for e in range(2):
                    c0, c1, s0, s1 = (
                        res[b * 32 : b * 32 + 32, e * 128 : e * 128 + 128] for b in range(4)
                    )
                    re = jnp.where(lo, c0, -s1) + swap(jnp.where(lo, c1, -s0))
                    im = jnp.where(lo, s0, c1) + swap(jnp.where(lo, s1, c0))
                    row = (pair * 2 + e) * 16 + dh
                    f_ref[pl.ds(row, NS, stride=64), :] = re
                    f_ref[pl.ds(row + 8, NS, stride=64), :] = im
            return carry

        lax.fori_loop(0, ND, go, 0, unroll=2)

        def narrow(t, carry):
            send_s[n_space, t] = (
                f_ref[pl.ds(pl.multiple_of(t * 64, 64), 64), :].astype(BF16).reshape(J, 16, LANES)
            )
            return carry

        lax.fori_loop(0, NS, narrow, 0, unroll=4)

    def y_inverse(n):
        def go(izh, carry):
            for pair in range(2):
                parts = [
                    jnp.concatenate(
                        [recv_s[n, iyl * 8 + izh, pair * 2 + e] for iyl in range(4)], axis=0
                    )
                    for e in range(2)
                ]
                res = dot(yi[...], jnp.concatenate(parts, axis=1))
                for e in range(2):
                    iz = izh * 4 + pair * 2 + e
                    a_ref[pl.ds(pl.multiple_of(iz * 128, 128), 128), :] = res[
                        :, e * 128 : e * 128 + 128
                    ]
            return carry

        lax.fori_loop(0, 8, go, 0, unroll=2)

    def z_inverse(table, q):
        rows = [a_ref[pl.ds(q * 4 + yl, 64, stride=64), :] for yl in range(4)]
        return dot(jnp.concatenate(rows, axis=0).astype(BF16), table[...], TN)

    def first(q, carry):
        cells = pl.ds(pl.multiple_of(q * 256, 256), 256)
        z_forward(x_ref[:, cells], zf, q)
        return carry

    lax.fori_loop(0, BLOCKS, first, 0, unroll=2)
    y_forward(0)
    pl.semaphore_wait(barrier, NS + ND - 2)
    exchange_space(0)
    arrived_space(0)
    x_forward(0, 0)
    exchange_dp(0)
    w_copy.wait()
    arrived_dp(0)

    widen_dp(0, v_ref)
    sign = jnp.where(lo, 1.0, -1.0).astype(F32)

    def twice(k, j):
        w = w_ref[k, j]
        return jnp.concatenate([w, w], axis=0)

    def mix(k, carry):
        for j in range(J):
            rows = pl.ds(j * M + k, ND, stride=128)
            v = v_ref[rows, :]
            lhs = jnp.concatenate([jnp.where(lo, v, 0.0), jnp.where(lo, 0.0, v)], axis=0)
            res = dot(lhs.astype(BF16), twice(k, j))
            m_ref[rows, :] = res[:ND] - swap(res[ND:]) * sign
        return carry

    lax.fori_loop(0, M, mix, 0, unroll=2)
    narrow_dp(1)
    exchange_dp(1)
    arrived_dp(1)
    x_inverse(1, 1)
    exchange_space(1)
    cot_copy.wait()
    arrived_space(1)
    y_inverse(1)

    def middle(q, carry):
        cells = pl.ds(pl.multiple_of(q * 256, 256), 256)
        pre = z_inverse(zih, q) + dot(mix_in[...], x_ref[:, cells]) + bias_ref[...]
        cdf = 0.5 * (1.0 + lax.erf(pre * math.sqrt(0.5)))
        out_ref[:, cells] = (pre * cdf).astype(BF16)
        pdf = jnp.exp(-0.5 * pre * pre) * (1.0 / math.sqrt(2.0 * math.pi))
        gp = (cot_ref[:, cells].astype(F32) * (cdf + pre * pdf)).astype(BF16)
        gp_ref[:, cells] = gp
        return carry

    lax.fori_loop(0, BLOCKS, middle, 0)
    out_copy = pltpu.make_async_copy(out_ref, out_hbm, sem_local.at[2])
    out_copy.start()

    def second(q, carry):
        cells = pl.ds(pl.multiple_of(q * 256, 256), 256)
        z_forward(gp_ref[:, cells], zfh, q)
        return carry

    lax.fori_loop(0, BLOCKS, second, 0, unroll=2)
    y_forward(2)
    exchange_space(2)
    arrived_space(2)
    x_forward(2, 2)
    exchange_dp(2)
    arrived_dp(2)
    widen_dp(2, u_ref)

    def mix_grad(k, carry):
        for j in range(J):
            rows = pl.ds(j * M + k, ND, stride=128)
            g = u_ref[rows, :]
            lhs = jnp.concatenate([g, swap(g) * sign], axis=0)
            res = dot(lhs.astype(BF16), twice(k, j), NT)
            m_ref[rows, :] = jnp.where(lo, res[:ND], res[ND:])
        return carry

    lax.fori_loop(0, M, mix_grad, 0, unroll=2)
    narrow_dp(3)
    exchange_dp(3)

    def weight_grad(k, carry):
        for j in range(J):
            rows = pl.ds(j * M + k, ND, stride=128)
            v = v_ref[rows, :]
            g = u_ref[rows, :]
            lhs = jnp.concatenate([v, swap(v)], axis=0).astype(BF16)
            rhs = jnp.concatenate([g, swap(g) * sign], axis=0).astype(BF16)
            gw_ref[k, j] = dot(lhs[:, :64], rhs, TN)
        return carry

    lax.fori_loop(0, M, weight_grad, 0)
    gw_copy = pltpu.make_async_copy(gw_ref, gw_hbm, sem_local.at[3])
    gw_copy.start()

    arrived_dp(3)
    x_inverse(3, 3)
    exchange_space(3)
    arrived_space(3)
    y_inverse(3)

    def last(q, carry):
        cells = pl.ds(pl.multiple_of(q * 256, 256), 256)
        gin_ref[:, cells] = (z_inverse(zi, q) + dot(mix_back[...], gp_ref[:, cells])).astype(BF16)
        return carry

    lax.fori_loop(0, BLOCKS, last, 0)
    gin_copy = pltpu.make_async_copy(gin_ref, gin_hbm, sem_local.at[4])
    gin_copy.start()

    for n in range(4):
        sent = send_s.at[n, pl.ds(0, NS - 1)]
        pltpu.make_async_copy(sent, sent, sem_send_s.at[n]).wait()
        sent = send_d.at[n, pl.ds(0, ND - 1)]
        pltpu.make_async_copy(sent, sent, sem_send_d.at[n]).wait()
    out_copy.wait()
    gw_copy.wait()
    gin_copy.wait()


def local(fields, spec_weights, local_weight, bias, cotangent):
    x = fields.reshape(LANES, G * G)
    cot = cotangent.reshape(LANES, G * G)
    zero = jnp.zeros_like(local_weight)
    mix_back = jnp.block([[local_weight, zero], [zero, local_weight]])
    mix_in = mix_back.T
    bias2 = jnp.tile(bias, 2)[:, None]
    vmem = pl.BlockSpec(memory_space=pltpu.VMEM)
    hbm = pl.BlockSpec(memory_space=pl.ANY)
    consts = [jnp.asarray(t) for t in tables()]
    out, gin, gw = pl.pallas_call(
        kernel,
        out_shape=(
            jax.ShapeDtypeStruct(x.shape, BF16),
            jax.ShapeDtypeStruct(x.shape, BF16),
            jax.ShapeDtypeStruct(spec_weights.shape, F32),
        ),
        in_specs=[vmem] * 12 + [hbm] * 2,
        out_specs=(hbm, hbm, hbm),
        scratch_shapes=[
            pltpu.VMEM((M, J, 64, 128), BF16),
            pltpu.VMEM((LANES, G * G), BF16),
            pltpu.VMEM((LANES, G * G), BF16),
            pltpu.VMEM((LANES, G * G), BF16),
            pltpu.VMEM((LANES, G * G), BF16),
            pltpu.VMEM((M, J, 64, 128), F32),
            pltpu.VMEM((4096, LANES), F32),
            pltpu.VMEM((2048, LANES), F32),
            pltpu.VMEM((1024, LANES), F32),
            pltpu.VMEM((1024, LANES), F32),
            pltpu.VMEM((1024, LANES), F32),
            pltpu.VMEM((4, NS, J, 16, LANES), BF16),
            pltpu.VMEM((4, NS, J, 16, LANES), BF16),
            pltpu.VMEM((4, ND, J, M, LANES), BF16),
            pltpu.VMEM((4, ND, J, M, LANES), BF16),
            pltpu.SemaphoreType.DMA((4,)),
            pltpu.SemaphoreType.DMA((4,)),
            pltpu.SemaphoreType.DMA((4,)),
            pltpu.SemaphoreType.DMA((4,)),
            pltpu.SemaphoreType.DMA((5,)),
        ],
        compiler_params=pltpu.CompilerParams(
            collective_id=0, has_side_effects=True, vmem_limit_bytes=48 * 2**20
        ),
        cost_estimate=pl.CostEstimate(
            flops=2 * 10**9, bytes_accessed=12 * 2**20, transcendentals=2 * 10**6
        ),
    )(x, mix_in, mix_back, bias2, *consts, spec_weights, cot)
    shape = fields.shape
    return out.reshape(shape), gin.reshape(shape), gw


def solution(mesh):
    placed = (
        P("dp", "space", None, None),
        P(None, ("dp", "space"), None, None),
        P(),
        P(),
        P("dp", "space", None, None),
    )
    return jax.shard_map(
        local,
        mesh=mesh,
        in_specs=placed,
        out_specs=(
            P("dp", "space", None, None),
            P("dp", "space", None, None),
            P(None, ("dp", "space"), None, None),
        ),
        check_vma=False,
    )
```

```python
import functools
import math

import jax
import jax.numpy as jnp
import ml_dtypes
import numpy as np
from jax import lax
from jax.experimental import pallas as pl
from jax.experimental.pallas import tpu as pltpu
from jax.sharding import PartitionSpec as P

MESH = pl.DeviceIdType.MESH
BF16 = jnp.bfloat16
F32 = jnp.float32

G = 64
M = 32
NS = 32
ND = 8
J = 4
LANES = 128
BLOCKS = 16

NT = (((1,), (1,)), ((), ()))
TN = (((0,), (0,)), ((), ()))


def tables():
    step = 2.0 * math.pi / G
    cell = np.arange(G)
    freq_z = np.arange(M)
    signed = np.where(np.arange(M) < M // 2, np.arange(M), G - M + np.arange(M))
    halves = np.where(freq_z == 0, 1.0, 2.0)
    angle = (freq_z[:, None] * cell[None, :] % G) * step
    z_rows = np.concatenate([np.cos(angle), -np.sin(angle)]) / 8
    z_rows_half = z_rows * np.tile(halves, 2)[:, None]
    four = np.eye(4)
    z_forward = np.kron(four, z_rows)
    z_forward_half = np.kron(four, z_rows_half)
    inv = np.stack([np.cos(angle), -np.sin(angle)], axis=1).reshape(2 * M, G) / 8
    inv_half = inv * np.repeat(halves, 2)[:, None]
    z_inverse = np.kron(four, inv)
    z_inverse_half = np.kron(four, inv_half)
    iy = np.arange(ND)[None, :] * 4 + np.arange(4)[:, None]
    ang_y = (signed[iy][:, :, None] * cell % G) * step
    c, s = np.cos(ang_y) / 8, np.sin(ang_y) / 8
    y_forward = np.stack([np.stack([c, s], -1), np.stack([-s, c], -1)], 1).reshape(64, 128)
    ct, st = c.transpose(2, 0, 1), s.transpose(2, 0, 1)
    y_inverse = np.stack([np.stack([ct, -st], 2), np.stack([st, ct], 2)], 0).reshape(128, 64)
    xs = 2 * np.arange(NS)[None, :] + np.arange(2)[:, None]
    ang_x = (signed[None, :, None] * xs[:, None, :] % G) * step
    c, s = np.cos(ang_x) / 8, np.sin(ang_x) / 8
    x_forward = np.stack([np.stack([c, s], 2), np.stack([-s, c], 2)], 1)
    x_forward = x_forward.reshape(128, 64)
    x_inverse = np.stack([c.transpose(0, 2, 1), s.transpose(0, 2, 1)]).reshape(128, M)
    return [
        t.astype(np.float32).astype(ml_dtypes.bfloat16)
        for t in (
            z_forward, z_forward_half, z_inverse, z_inverse_half,
            y_forward, y_inverse, x_forward, x_inverse,
        )
    ]


def dot(a, b, dims=(((1,), (0,)), ((), ()))):
    return lax.dot_general(a, b, dims, preferred_element_type=F32)


def kernel(
    x_hbm, weight_hbm, bias_hbm, z_hbm, small_hbm, w_hbm, cot_hbm,
    out_hbm, gin_hbm, gw_hbm,
    x_ref, weight_ref, bias_ref, z_ref, small_ref, mix_ref,
    w_ref, cot_ref, out_ref, gp_ref, gin_ref, gw_ref,
    a_ref, e_ref, f_ref, v_ref, u_ref, m_ref,
    send_s, recv_s, send_d, recv_d,
    sem_send_s, sem_recv_s, sem_send_d, sem_recv_d, sem_local, sem_x,
):
    d = lax.axis_index("dp")
    s = lax.axis_index("space")

    def fetch(src, dst, sem):
        copy = pltpu.make_async_copy(src, dst, sem)
        copy.start()
        return copy

    quarter = G * G // 4
    z_copy = fetch(z_hbm, z_ref, sem_local.at[0])
    x_copies = [
        fetch(
            x_hbm.at[:, pl.ds(i * quarter, quarter)],
            x_ref.at[:, pl.ds(i * quarter, quarter)],
            sem_x.at[i],
        )
        for i in range(4)
    ]
    small_copy = fetch(small_hbm, small_ref, sem_local.at[1])
    weight_copy = fetch(weight_hbm, weight_ref, sem_local.at[2])
    bias_copy = fetch(bias_hbm, bias_ref, sem_local.at[3])
    w_copy = fetch(w_hbm, w_ref, sem_local.at[4])
    cot_copy = fetch(cot_hbm, cot_ref, sem_local.at[5])

    barrier = pltpu.get_barrier_semaphore()

    def greet_space(i, carry):
        pl.semaphore_signal(barrier, inc=1, device_id=(d, lax.rem(s + i, NS)), device_id_type=MESH)
        return carry

    def greet_dp(i, carry):
        pl.semaphore_signal(barrier, inc=1, device_id=(lax.rem(d + i, ND), s), device_id_type=MESH)
        return carry

    lax.fori_loop(1, NS, greet_space, 0)
    lax.fori_loop(1, ND, greet_dp, 0)

    lo = lax.broadcasted_iota(jnp.int32, (1, LANES), 1) < 64
    sign = jnp.where(lo, 1.0, -1.0).astype(F32)

    def swap(v):
        return pltpu.roll(v, 64, 1)

    def exchange_space(n, c):
        src, dst = send_s.at[n, c], recv_s.at[n, c]

        def go(i, carry):
            t = lax.rem(s + i, NS)
            pltpu.make_async_remote_copy(
                src_ref=src.at[t], dst_ref=dst.at[s],
                send_sem=sem_send_s.at[n, c], recv_sem=sem_recv_s.at[n, c],
                device_id=(d, t), device_id_type=MESH,
            ).start()
            return carry

        lax.fori_loop(1, NS, go, 0)
        pltpu.make_async_copy(src.at[s], dst.at[s], sem_recv_s.at[n, c]).start()

    def exchange_dp(n, c):
        src, dst = send_d.at[n, c], recv_d.at[n, c]

        def go(i, carry):
            t = lax.rem(d + i, ND)
            pltpu.make_async_remote_copy(
                src_ref=src.at[t], dst_ref=dst.at[d],
                send_sem=sem_send_d.at[n, c], recv_sem=sem_recv_d.at[n, c],
                device_id=(t, s), device_id_type=MESH,
            ).start()
            return carry

        lax.fori_loop(1, ND, go, 0)
        pltpu.make_async_copy(src.at[d], dst.at[d], sem_recv_d.at[n, c]).start()

    def arrived_space(n, c):
        pltpu.make_async_copy(recv_s.at[n, c], recv_s.at[n, c], sem_recv_s.at[n, c]).wait()

    def arrived_dp(n, c):
        pltpu.make_async_copy(recv_d.at[n, c], recv_d.at[n, c], sem_recv_d.at[n, c]).wait()

    def chunks(step):
        def go(c, carry):
            step(c)
            return carry

        lax.fori_loop(0, J, go, 0)

    def z_forward(block, table, q, to):
        to[pl.ds(pl.multiple_of(q * 256, 256), 256), :] = dot(z_ref[table], block, NT)

    def y_forward(n, c, source):
        table = small_ref[0, :64, :]
        for pair in range(4):
            parts = [
                source[pl.ds((pair * 2 + e) * 4 + c, 128, stride=M), :].astype(BF16)
                for e in range(2)
            ]
            res = dot(table, jnp.concatenate(parts, axis=1)).astype(BF16)
            for e in range(2):
                for iyl in range(4):
                    send_s[n, c, iyl * 8 + pair * 2 + e] = res[
                        iyl * 16 : iyl * 16 + 16, e * 128 : e * 128 + 128
                    ]

    def x_forward(n_space, n_dp, c):
        f_ref[...] = recv_s[n_space, c].reshape(NS * 16, LANES).astype(F32)
        table = small_ref[2, :, :64]
        for pair in range(4):
            parts = []
            for e in range(2):
                row = pair * 2 + e
                parts.append(
                    jnp.concatenate(
                        [
                            f_ref[pl.ds(row, NS, stride=16), :],
                            f_ref[pl.ds(row + 8, NS, stride=16), :],
                        ],
                        axis=0,
                    ).astype(BF16)
                )
            res = dot(table, jnp.concatenate(parts, axis=1))
            for e in range(2):
                p00, p01, p10, p11 = (
                    res[b * 32 : b * 32 + 32, e * 128 : e * 128 + 128] for b in range(4)
                )
                both = jnp.where(lo, p00, p11) + swap(jnp.where(lo, p01, p10))
                send_d[n_dp, c, pair * 2 + e] = both.astype(BF16)

    def widen_dp(n, c, to):
        to[c] = recv_d[n, c].reshape(ND * M, LANES).astype(F32)

    def narrow_dp(n, c):
        send_d[n, c] = m_ref[...].astype(BF16).reshape(ND, M, LANES)

    def x_inverse(n_dp, n_space, c):
        table = small_ref[3, :, :M]
        for pair in range(4):
            rhs = jnp.concatenate(
                [recv_d[n_dp, c, pair * 2], recv_d[n_dp, c, pair * 2 + 1]], axis=1
            )
            res = dot(table, rhs)
            for e in range(2):
                c0, c1, s0, s1 = (
                    res[b * 32 : b * 32 + 32, e * 128 : e * 128 + 128] for b in range(4)
                )
                row = pair * 2 + e
                f_ref[pl.ds(row, NS, stride=16), :] = jnp.where(lo, c0, -s1) + swap(
                    jnp.where(lo, c1, -s0)
                )
                f_ref[pl.ds(row + 8, NS, stride=16), :] = jnp.where(lo, s0, c1) + swap(
                    jnp.where(lo, s1, c0)
                )
        send_s[n_space, c] = f_ref[...].astype(BF16).reshape(NS, 16, LANES)

    def y_inverse(n, c):
        table = small_ref[1, :, :64]
        for pair in range(4):
            parts = [
                jnp.concatenate(
                    [recv_s[n, c, iyl * 8 + pair * 2 + e] for iyl in range(4)], axis=0
                )
                for e in range(2)
            ]
            res = dot(table, jnp.concatenate(parts, axis=1))
            for e in range(2):
                iz = (pair * 2 + e) * 4 + c
                a_ref[pl.ds(pl.multiple_of(iz * 128, 128), 128), :] = res[
                    :, e * 128 : e * 128 + 128
                ]

    def z_inverse(table, q):
        rows = [a_ref[pl.ds(q * 4 + yl, 64, stride=64), :] for yl in range(4)]
        return dot(jnp.concatenate(rows, axis=0).astype(BF16), z_ref[table], TN)

    z_copy.wait()
    for i in range(4):
        x_copies[i].wait()
        for q in range(4 * i, 4 * i + 4):
            z_forward(x_ref[:, q * 256 : q * 256 + 256], 0, q, e_ref)
    small_copy.wait()
    weight_copy.wait()
    bias_copy.wait()

    weight = weight_ref[...].astype(F32)
    zero = jnp.zeros((64, 64), F32)
    both = jnp.concatenate(
        [jnp.concatenate([weight, zero], axis=1), jnp.concatenate([zero, weight], axis=1)], axis=0
    )
    mix_ref[0] = both.T.astype(BF16)
    mix_ref[1] = both.astype(BF16)
    diagonal = lax.broadcasted_iota(jnp.int32, (64, 64), 0) == lax.broadcasted_iota(
        jnp.int32, (64, 64), 1
    )
    column = jnp.sum(jnp.where(diagonal, bias_ref[...], 0.0), axis=1, keepdims=True)
    bias = jnp.concatenate([column, column], axis=0)

    pl.semaphore_wait(barrier, NS + ND - 2)

    def out_space(n):
        def step(c):
            y_forward(n, c, e_ref)
            exchange_space(n, c)

        chunks(step)

    def out_dp(n):
        def step(c):
            arrived_space(n, c)
            x_forward(n, n, c)
            exchange_dp(n, c)

        chunks(step)

    def back_space(n):
        def step(c):
            arrived_dp(n, c)
            x_inverse(n, n, c)
            exchange_space(n, c)

        chunks(step)

    def back_grid(n):
        def step(c):
            arrived_space(n, c)
            y_inverse(n, c)

        chunks(step)

    out_space(0)
    out_dp(0)

    w_copy.wait()

    def twice(k, j):
        w = w_ref[k, j]
        return jnp.concatenate([w, w], axis=0)

    def mix(j):
        arrived_dp(0, j)
        widen_dp(0, j, v_ref)

        def go(k, carry):
            rows = pl.ds(k, ND, stride=M)
            v = v_ref[j, rows, :]
            lhs = jnp.concatenate([jnp.where(lo, v, 0.0), jnp.where(lo, 0.0, v)], axis=0)
            res = dot(lhs.astype(BF16), twice(k, j))
            m_ref[rows, :] = res[:ND] - swap(res[ND:]) * sign
            return carry

        lax.fori_loop(0, M, go, 0, unroll=8)
        narrow_dp(1, j)
        exchange_dp(1, j)

    chunks(mix)
    back_space(1)
    cot_copy.wait()
    back_grid(1)

    def middle(q, carry):
        cells = pl.ds(pl.multiple_of(q * 256, 256), 256)
        pre = z_inverse(3, q) + dot(mix_ref[0], x_ref[:, cells]) + bias
        cdf = 0.5 * (1.0 + lax.erf(pre * math.sqrt(0.5)))
        out_ref[:, cells] = (pre * cdf).astype(BF16)
        pdf = jnp.exp(-0.5 * pre * pre) * (1.0 / math.sqrt(2.0 * math.pi))
        gp = (cot_ref[:, cells].astype(F32) * (cdf + pre * pdf)).astype(BF16)
        gp_ref[:, cells] = gp
        z_forward(gp, 1, q, e_ref)
        return carry

    lax.fori_loop(0, BLOCKS, middle, 0, unroll=2)
    out_copy = fetch(out_ref, out_hbm, sem_local.at[6])

    out_space(2)
    out_dp(2)

    def mix_grad(j):
        arrived_dp(2, j)
        widen_dp(2, j, u_ref)

        def go(k, carry):
            rows = pl.ds(k, ND, stride=M)
            g = u_ref[j, rows, :]
            lhs = jnp.concatenate([g, swap(g) * sign], axis=0)
            res = dot(lhs.astype(BF16), twice(k, j), NT)
            m_ref[rows, :] = jnp.where(lo, res[:ND], res[ND:])
            return carry

        lax.fori_loop(0, M, go, 0, unroll=8)
        narrow_dp(3, j)
        exchange_dp(3, j)

    chunks(mix_grad)

    def weight_grad(j):
        def go(k, carry):
            rows = pl.ds(k, ND, stride=M)
            v = v_ref[j, rows, :]
            g = u_ref[j, rows, :]
            lhs = jnp.concatenate([v, swap(v)], axis=0).astype(BF16)
            rhs = jnp.concatenate([g, swap(g) * sign], axis=0).astype(BF16)
            gw_ref[k, j] = dot(lhs[:, :64], rhs, TN)
            return carry

        lax.fori_loop(0, M, go, 0, unroll=8)

    def back_space_grad(c):
        arrived_dp(3, c)
        x_inverse(3, 3, c)
        exchange_space(3, c)
        weight_grad(c)

    chunks(back_space_grad)
    gw_copy = fetch(gw_ref, gw_hbm, sem_local.at[7])
    back_grid(3)

    def last(q, carry):
        cells = pl.ds(pl.multiple_of(q * 256, 256), 256)
        gin_ref[:, cells] = (z_inverse(2, q) + dot(mix_ref[1], gp_ref[:, cells])).astype(BF16)
        return carry

    lax.fori_loop(0, BLOCKS, last, 0, unroll=2)
    gin_copy = fetch(gin_ref, gin_hbm, sem_local.at[8])

    for n in range(4):

        def sent(c, n=n):
            part = send_s.at[n, c, pl.ds(0, NS - 1)]
            pltpu.make_async_copy(part, part, sem_send_s.at[n, c]).wait()
            part = send_d.at[n, c, pl.ds(0, ND - 1)]
            pltpu.make_async_copy(part, part, sem_send_d.at[n, c]).wait()

        chunks(sent)
    out_copy.wait()
    gw_copy.wait()
    gin_copy.wait()


def local(fields, spec_weights, local_weight, bias, cotangent):
    x = fields.reshape(LANES, G * G)
    cot = cotangent.reshape(LANES, G * G)
    made = tables()
    z_tables = jnp.asarray(np.stack(made[:4]))
    small = np.zeros((4, 128, 128), ml_dtypes.bfloat16)
    for i, t in enumerate(made[4:]):
        small[i, : t.shape[0], : t.shape[1]] = t
    hbm = pl.BlockSpec(memory_space=pltpu.HBM)
    out, gin, gw = pl.pallas_call(
        kernel,
        out_shape=(
            jax.ShapeDtypeStruct(x.shape, BF16),
            jax.ShapeDtypeStruct(x.shape, BF16),
            jax.ShapeDtypeStruct(spec_weights.shape, F32),
        ),
        in_specs=[hbm] * 7,
        out_specs=(hbm, hbm, hbm),
        scratch_shapes=[
            pltpu.VMEM((LANES, G * G), BF16),
            pltpu.VMEM((64, 64), BF16),
            pltpu.VMEM((1, 64), F32),
            pltpu.VMEM((4, 256, 256), BF16),
            pltpu.VMEM((4, 128, 128), BF16),
            pltpu.VMEM((2, 128, 128), BF16),
            pltpu.VMEM((M, J, 64, 128), BF16),
            pltpu.VMEM((LANES, G * G), BF16),
            pltpu.VMEM((LANES, G * G), BF16),
            pltpu.VMEM((LANES, G * G), BF16),
            pltpu.VMEM((LANES, G * G), BF16),
            pltpu.VMEM((M, J, 64, 128), F32),
            pltpu.VMEM((4096, LANES), F32),
            pltpu.VMEM((4096, LANES), F32),
            pltpu.VMEM((NS * 16, LANES), F32),
            pltpu.VMEM((J, ND * M, LANES), F32),
            pltpu.VMEM((J, ND * M, LANES), F32),
            pltpu.VMEM((ND * M, LANES), F32),
            pltpu.VMEM((4, J, NS, 16, LANES), BF16),
            pltpu.VMEM((4, J, NS, 16, LANES), BF16),
            pltpu.VMEM((4, J, ND, M, LANES), BF16),
            pltpu.VMEM((4, J, ND, M, LANES), BF16),
            pltpu.SemaphoreType.DMA((4, J)),
            pltpu.SemaphoreType.DMA((4, J)),
            pltpu.SemaphoreType.DMA((4, J)),
            pltpu.SemaphoreType.DMA((4, J)),
            pltpu.SemaphoreType.DMA((9,)),
            pltpu.SemaphoreType.DMA((4,)),
        ],
        compiler_params=pltpu.CompilerParams(
            collective_id=0, has_side_effects=True, vmem_limit_bytes=63 * 2**20
        ),
        cost_estimate=pl.CostEstimate(
            flops=2 * 10**9, bytes_accessed=12 * 2**20, transcendentals=2 * 10**6
        ),
    )(x, local_weight, bias.reshape(1, 64), z_tables, jnp.asarray(small), spec_weights, cot)
    shape = fields.shape
    return out.reshape(shape), gin.reshape(shape), gw


def solution(mesh):
    placed = (
        P("dp", "space", None, None),
        P(None, ("dp", "space"), None, None),
        P(),
        P(),
        P("dp", "space", None, None),
    )
    return jax.shard_map(
        local,
        mesh=mesh,
        in_specs=placed,
        out_specs=(
            P("dp", "space", None, None),
            P("dp", "space", None, None),
            P(None, ("dp", "space"), None, None),
        ),
        check_vma=False,
    )
```

```python
import functools
import math

import jax
import jax.numpy as jnp
import ml_dtypes
import numpy as np
from jax import lax
from jax.experimental import pallas as pl
from jax.experimental.pallas import tpu as pltpu
from jax.sharding import PartitionSpec as P

MESH = pl.DeviceIdType.MESH
BF16 = jnp.bfloat16
F32 = jnp.float32

G = 64
M = 32
NS = 32
ND = 8
J = 4
LANES = 128
BLOCKS = 16

NT = (((1,), (1,)), ((), ()))
TN = (((0,), (0,)), ((), ()))


def tables():
    step = 2.0 * math.pi / G
    cell = np.arange(G)
    freq_z = np.arange(M)
    signed = np.where(np.arange(M) < M // 2, np.arange(M), G - M + np.arange(M))
    halves = np.where(freq_z == 0, 1.0, 2.0)
    angle = (freq_z[:, None] * cell[None, :] % G) * step
    z_rows = np.concatenate([np.cos(angle), -np.sin(angle)]) / 8
    z_rows_half = z_rows * np.tile(halves, 2)[:, None]
    four = np.eye(4)
    z_forward = np.kron(four, z_rows)
    z_forward_half = np.kron(four, z_rows_half)
    inv = np.stack([np.cos(angle), -np.sin(angle)], axis=1).reshape(2 * M, G) / 8
    inv_half = inv * np.repeat(halves, 2)[:, None]
    z_inverse, z_inverse_half = (
        np.kron(four, t).reshape(4, ND, J, 2, 256).transpose(2, 0, 1, 3, 4).reshape(J, 64, 256)
        for t in (inv, inv_half)
    )
    iy = np.arange(ND)[None, :] * 4 + np.arange(4)[:, None]
    ang_y = (signed[iy][:, :, None] * cell % G) * step
    c, s = np.cos(ang_y) / 8, np.sin(ang_y) / 8
    y_forward = np.stack([np.stack([c, s], -1), np.stack([-s, c], -1)], 1).reshape(64, 128)
    ct, st = c.transpose(2, 0, 1), s.transpose(2, 0, 1)
    y_inverse = np.stack([np.stack([ct, -st], 2), np.stack([st, ct], 2)], 0).reshape(128, 64)
    xs = 2 * np.arange(NS)[None, :] + np.arange(2)[:, None]
    ang_x = (signed[None, :, None] * xs[:, None, :] % G) * step
    c, s = np.cos(ang_x) / 8, np.sin(ang_x) / 8
    x_forward = np.stack([np.stack([c, s], 2), np.stack([-s, c], 2)], 1)
    x_forward = x_forward.reshape(128, 64)
    x_inverse = np.stack([c.transpose(0, 2, 1), s.transpose(0, 2, 1)]).reshape(128, M)
    return [
        t.astype(np.float32).astype(ml_dtypes.bfloat16)
        for t in (
            z_forward, z_forward_half, z_inverse, z_inverse_half,
            y_forward, y_inverse, x_forward, x_inverse,
        )
    ]


def dot(a, b, dims=(((1,), (0,)), ((), ()))):
    return lax.dot_general(a, b, dims, preferred_element_type=F32)


def farthest_first():
    def ring(i, n):
        return min(i, n - i)

    offsets = [(y, x, c) for y in range(4) for x in range(4) for c in range(2)][1:]
    offsets.sort(key=lambda o: -ring(o[0], 4) - ring(o[1], 4))
    return offsets, sorted(range(1, ND), key=lambda i: -ring(i, ND))


def kernel(
    x_hbm, weight_hbm, bias_hbm, zf_hbm, zi_hbm, small_hbm, w_hbm, cot_hbm,
    out_ref, gw_ref, acc_ref, a_ref, last_ref,
    x_ref, weight_ref, bias_ref, zf_ref, zi_ref, small_ref, mix_ref,
    w_ref, cot_ref, gp_ref,
    e_ref, f_ref, v_ref, u_ref, m_ref,
    send_s, recv_s, send_d, recv_d,
    sem_send_s, sem_recv_s, sem_send_d, sem_recv_d, sem_local, sem_x,
):
    d = lax.axis_index("dp")
    s = lax.axis_index("space")
    row_y, row_x, core = s // 8, lax.rem(s // 2, 4), lax.rem(s, 2)
    space_offsets, dp_offsets = farthest_first()

    def fetch(src, dst, sem):
        copy = pltpu.make_async_copy(src, dst, sem)
        copy.start()
        return copy

    quarter = G * G // 4
    zf_copy = fetch(zf_hbm, zf_ref, sem_local.at[0])
    x_copies = [
        fetch(
            x_hbm.at[:, pl.ds(i * quarter, quarter)],
            x_ref.at[:, pl.ds(i * quarter, quarter)],
            sem_x.at[i],
        )
        for i in range(4)
    ]
    small_copy = fetch(small_hbm, small_ref, sem_local.at[1])
    weight_copy = fetch(weight_hbm, weight_ref, sem_local.at[2])
    bias_copy = fetch(bias_hbm, bias_ref, sem_local.at[3])
    zi_copy = fetch(zi_hbm, zi_ref, sem_local.at[4])
    w_copy = fetch(w_hbm, w_ref, sem_local.at[5])
    cot_copy = fetch(cot_hbm, cot_ref, sem_local.at[6])

    barrier = pltpu.get_barrier_semaphore()

    def greet_space(i, carry):
        pl.semaphore_signal(barrier, inc=1, device_id=(d, lax.rem(s + i, NS)), device_id_type=MESH)
        return carry

    def greet_dp(i, carry):
        pl.semaphore_signal(barrier, inc=1, device_id=(lax.rem(d + i, ND), s), device_id_type=MESH)
        return carry

    lax.fori_loop(1, ND, greet_dp, 0)
    lax.fori_loop(1, NS, greet_space, 0)

    lo = lax.broadcasted_iota(jnp.int32, (1, LANES), 1) < 64
    sign = jnp.where(lo, 1.0, -1.0).astype(F32)

    def swap(v):
        return pltpu.roll(v, 64, 1)

    def exchange_space(n, c):
        src, dst = send_s.at[n, c], recv_s.at[n, c]
        for oy, ox, oc in space_offsets:
            t = lax.rem(row_y + oy, 4) * 8 + lax.rem(row_x + ox, 4) * 2 + lax.rem(core + oc, 2)
            pltpu.make_async_remote_copy(
                src_ref=src.at[t], dst_ref=dst.at[s],
                send_sem=sem_send_s.at[n, c], recv_sem=sem_recv_s.at[n, c],
                device_id=(d, t), device_id_type=MESH,
            ).start()
        pltpu.make_async_copy(src.at[s], dst.at[s], sem_recv_s.at[n, c]).start()

    def exchange_dp(n, g):
        src, dst = send_d.at[n, g], recv_d.at[n, g]
        for offset in dp_offsets:
            t = lax.rem(d + offset, ND)
            pltpu.make_async_remote_copy(
                src_ref=src.at[t], dst_ref=dst.at[d],
                send_sem=sem_send_d.at[n, g], recv_sem=sem_recv_d.at[n, g],
                device_id=(t, s), device_id_type=MESH,
            ).start()
        pltpu.make_async_copy(src.at[d], dst.at[d], sem_recv_d.at[n, g]).start()

    def arrived_space(n, c):
        pltpu.make_async_copy(recv_s.at[n, c], recv_s.at[n, c], sem_recv_s.at[n, c]).wait()

    def arrived_dp(n, g):
        pltpu.make_async_copy(recv_d.at[n, g], recv_d.at[n, g], sem_recv_d.at[n, g]).wait()

    def chunks(step, first=0, end=J):
        def go(c, carry):
            step(c)
            return carry

        lax.fori_loop(first, end, go, 0)

    def z_forward(block, table, q):
        e_ref[pl.ds(pl.multiple_of(q * 256, 256), 256), :] = dot(zf_ref[table], block, NT)

    def y_forward(n, c):
        table = small_ref[0, :64, :]
        for pair in range(4):
            parts = [
                e_ref[pl.ds((pair * 2 + e) * 4 + c, 128, stride=M), :].astype(BF16)
                for e in range(2)
            ]
            res = dot(table, jnp.concatenate(parts, axis=1)).astype(BF16)
            for e in range(2):
                for iyl in range(4):
                    send_s[n, c, iyl * 8 + pair * 2 + e] = res[
                        iyl * 16 : iyl * 16 + 16, e * 128 : e * 128 + 128
                    ]

    def x_forward(n_space, n_dp, c):
        f_ref[...] = recv_s[n_space, c].reshape(NS * 16, LANES).astype(F32)
        table = small_ref[2, :, :64]
        for pair in range(4):
            parts = []
            for e in range(2):
                row = pair * 2 + e
                parts.append(
                    jnp.concatenate(
                        [
                            f_ref[pl.ds(row, NS, stride=16), :],
                            f_ref[pl.ds(row + 8, NS, stride=16), :],
                        ],
                        axis=0,
                    ).astype(BF16)
                )
            res = dot(table, jnp.concatenate(parts, axis=1))
            for e in range(2):
                p00, p01, p10, p11 = (
                    res[b * 32 : b * 32 + 32, e * 128 : e * 128 + 128] for b in range(4)
                )
                both = jnp.where(lo, p00, p11) + swap(jnp.where(lo, p01, p10))
                both = both.astype(BF16)
                for h in range(2):
                    send_d[n_dp, c * 2 + h, pair * 2 + e] = both[h * 16 : h * 16 + 16]

    def widen_dp(n, g, to):
        to[g] = recv_d[n, g].reshape(ND * 16, LANES).astype(F32)

    def narrow_dp(n, g):
        send_d[n, g] = m_ref[...].astype(BF16).reshape(ND, 16, LANES)

    def x_inverse(n_dp, n_space, c):
        table = small_ref[3, :, :M]
        for pair in range(4):
            rhs = jnp.concatenate(
                [
                    jnp.concatenate(
                        [recv_d[n_dp, c * 2 + h, pair * 2 + e] for h in range(2)], axis=0
                    )
                    for e in range(2)
                ],
                axis=1,
            )
            res = dot(table, rhs)
            for e in range(2):
                c0, c1, s0, s1 = (
                    res[b * 32 : b * 32 + 32, e * 128 : e * 128 + 128] for b in range(4)
                )
                row = pair * 2 + e
                f_ref[pl.ds(row, NS, stride=16), :] = jnp.where(lo, c0, -s1) + swap(
                    jnp.where(lo, c1, -s0)
                )
                f_ref[pl.ds(row + 8, NS, stride=16), :] = jnp.where(lo, s0, c1) + swap(
                    jnp.where(lo, s1, c0)
                )
        send_s[n_space, c] = f_ref[...].astype(BF16).reshape(NS, 16, LANES)

    def y_inverse(n, c):
        table = small_ref[1, :, :64]
        for pair in range(4):
            parts = [
                jnp.concatenate(
                    [recv_s[n, c, iyl * 8 + pair * 2 + e] for iyl in range(4)], axis=0
                )
                for e in range(2)
            ]
            res = dot(table, jnp.concatenate(parts, axis=1))
            for e in range(2):
                izh = pair * 2 + e
                a_ref[izh * 128 : izh * 128 + 128, :] = res[:, e * 128 : e * 128 + 128]

    def cells(q):
        return pl.ds(pl.multiple_of(q * 256, 256), 256)

    zf_copy.wait()
    for i in range(4):
        x_copies[i].wait()
        for q in range(4 * i, 4 * i + 4):
            z_forward(x_ref[:, q * 256 : q * 256 + 256], 0, q)
    small_copy.wait()
    weight_copy.wait()
    bias_copy.wait()
    chunks(lambda c: y_forward(0, c))

    weight = weight_ref[...].astype(F32)
    zero = jnp.zeros((64, 64), F32)
    both = jnp.concatenate(
        [jnp.concatenate([weight, zero], axis=1), jnp.concatenate([zero, weight], axis=1)], axis=0
    )
    mix_ref[0] = both.T.astype(BF16)
    mix_ref[1] = both.astype(BF16)
    diagonal = lax.broadcasted_iota(jnp.int32, (64, 64), 0) == lax.broadcasted_iota(
        jnp.int32, (64, 64), 1
    )
    column = jnp.sum(jnp.where(diagonal, bias_ref[...], 0.0), axis=1, keepdims=True)
    bias = jnp.concatenate([column, column], axis=0)

    pl.semaphore_wait(barrier, NS + ND - 2)
    chunks(lambda c: exchange_space(0, c))

    def pointwise(q, carry):
        acc_ref[:, cells(q)] = dot(mix_ref[0], x_ref[:, cells(q)]) + bias
        return carry

    lax.fori_loop(0, BLOCKS, pointwise, 0, unroll=4)
    zi_copy.wait()
    last_ref[...] = zi_ref[0, J - 1]

    def out_dp(n):
        def step(c):
            arrived_space(n, c)
            x_forward(n, n, c)
            exchange_dp(n, c * 2)
            exchange_dp(n, c * 2 + 1)

        chunks(step)

    def back_space(n, c):
        arrived_dp(n, c * 2)
        arrived_dp(n, c * 2 + 1)
        x_inverse(n, n, c)
        exchange_space(n, c)

    def back_grid(n, table, c):
        arrived_space(n, c)
        y_inverse(n, c)

        def go(q, carry):
            acc_ref[:, cells(q)] += z_part(a_ref, zi_ref[table, c], q)
            return carry

        lax.fori_loop(0, BLOCKS, go, 0, unroll=4)

    out_dp(0)

    w_copy.wait()

    def twice(k, j):
        w = w_ref[k, j]
        return jnp.concatenate([w, w], axis=0)

    def mix(g):
        j, base = g // 2, lax.rem(g, 2) * 16
        arrived_dp(0, g)
        widen_dp(0, g, v_ref)

        def go(k, carry):
            rows = pl.ds(k, ND, stride=16)
            v = v_ref[g, rows, :]
            lhs = jnp.concatenate([jnp.where(lo, v, 0.0), jnp.where(lo, 0.0, v)], axis=0)
            res = dot(lhs.astype(BF16), twice(base + k, j))
            m_ref[rows, :] = res[:ND] - swap(res[ND:]) * sign
            return carry

        lax.fori_loop(0, 16, go, 0, unroll=16)
        narrow_dp(1, g)
        exchange_dp(1, g)

    chunks(mix, 0, 2 * J)
    chunks(lambda c: back_space(1, c))
    cot_copy.wait()
    chunks(lambda c: back_grid(1, 1, c), 0, J - 1)
    arrived_space(1, J - 1)
    y_inverse(1, J - 1)

    def middle(q, carry):
        pre = acc_ref[:, cells(q)] + z_part(a_ref, zi_ref[1, J - 1], q)
        cdf = 0.5 * (1.0 + lax.erf(pre * math.sqrt(0.5)))
        out_ref[:, cells(q)] = (pre * cdf).astype(BF16)
        pdf = jnp.exp(-0.5 * pre * pre) * (1.0 / math.sqrt(2.0 * math.pi))
        gp = (cot_ref[:, cells(q)].astype(F32) * (cdf + pre * pdf)).astype(BF16)
        gp_ref[:, cells(q)] = gp
        z_forward(gp, 1, q)
        return carry

    lax.fori_loop(0, BLOCKS, middle, 0, unroll=2)

    def out_space(c):
        y_forward(2, c)
        exchange_space(2, c)

    chunks(out_space)

    def pointwise_back(q, carry):
        acc_ref[:, cells(q)] = dot(mix_ref[1], gp_ref[:, cells(q)])
        return carry

    lax.fori_loop(0, BLOCKS, pointwise_back, 0, unroll=4)
    out_dp(2)

    def mix_grad(g):
        j, base = g // 2, lax.rem(g, 2) * 16
        arrived_dp(2, g)
        widen_dp(2, g, u_ref)

        def go(k, carry):
            rows = pl.ds(k, ND, stride=16)
            v = u_ref[g, rows, :]
            lhs = jnp.concatenate([v, swap(v) * sign], axis=0)
            res = dot(lhs.astype(BF16), twice(base + k, j), NT)
            m_ref[rows, :] = jnp.where(lo, res[:ND], res[ND:])
            return carry

        lax.fori_loop(0, 16, go, 0, unroll=16)
        narrow_dp(3, g)
        exchange_dp(3, g)

    chunks(mix_grad, 0, 2 * J)

    def weight_grad(g):
        j, base = g // 2, lax.rem(g, 2) * 16

        def go(k, carry):
            rows = pl.ds(k, ND, stride=16)
            v = v_ref[g, rows, :]
            grad = u_ref[g, rows, :]
            lhs = jnp.concatenate([v, swap(v)], axis=0).astype(BF16)
            rhs = jnp.concatenate([grad, swap(grad) * sign], axis=0).astype(BF16)
            gw_ref[base + k, j] = dot(lhs[:, :64], rhs, TN)
            return carry

        lax.fori_loop(0, 16, go, 0, unroll=8)

    def back_space_grad(c):
        back_space(3, c)
        weight_grad(c)

    chunks(back_space_grad, 0, 3)
    back_space(3, 3)

    def back_grid_grad(c):
        weight_grad(c * 2 + 3)
        back_grid(3, 0, c)
        weight_grad(c * 2 + 4)

    chunks(back_grid_grad, 0, 2)
    weight_grad(7)
    back_grid(3, 0, 2)
    arrived_space(3, J - 1)
    y_inverse(3, J - 1)

    for n in range(4):

        def sent_space(c, n=n):
            part = send_s.at[n, c, pl.ds(0, NS - 1)]
            pltpu.make_async_copy(part, part, sem_send_s.at[n, c]).wait()

        def sent_dp(g, n=n):
            part = send_d.at[n, g, pl.ds(0, ND - 1)]
            pltpu.make_async_copy(part, part, sem_send_d.at[n, g]).wait()

        chunks(sent_space)
        chunks(sent_dp, 0, 2 * J)


def z_part(a_ref, table, q):
    rows = [a_ref[pl.ds(q * 4 + yl, 16, stride=64), :] for yl in range(4)]
    return dot(jnp.concatenate(rows, axis=0).astype(BF16), table, TN)


def finish(
    out_ref, gw_ref, acc_ref, a_ref, last_ref,
    out_hbm, gin_hbm, gw_hbm,
    gin_ref, sem, sem_gin,
):
    copies = [
        pltpu.make_async_copy(gw_ref, gw_hbm, sem.at[0]),
        pltpu.make_async_copy(out_ref, out_hbm, sem.at[1]),
    ]
    for copy in copies:
        copy.start()
    quarter = G * G // 4
    for i in range(4):

        def last(q, carry):
            here = pl.ds(pl.multiple_of(q * 256, 256), 256)
            gin_ref[:, here] = (acc_ref[:, here] + z_part(a_ref, last_ref[...], q)).astype(BF16)
            return carry

        lax.fori_loop(4 * i, 4 * i + 4, last, 0, unroll=4)
        part = pl.ds(i * quarter, quarter)
        copy = pltpu.make_async_copy(gin_ref.at[:, part], gin_hbm.at[:, part], sem_gin.at[i])
        copy.start()
        copies.append(copy)
    for copy in copies:
        copy.wait()


def local(fields, spec_weights, local_weight, bias, cotangent):
    x = fields.reshape(LANES, G * G)
    cot = cotangent.reshape(LANES, G * G)
    made = tables()
    zf_tables = jnp.asarray(np.stack(made[0:2]))
    zi_tables = jnp.asarray(np.stack(made[2:4]))
    small = np.zeros((4, 128, 128), ml_dtypes.bfloat16)
    for i, t in enumerate(made[4:]):
        small[i, : t.shape[0], : t.shape[1]] = t
    hbm = pl.BlockSpec(memory_space=pltpu.HBM)
    vmem = pl.BlockSpec(memory_space=pltpu.VMEM)
    parts = pl.pallas_call(
        kernel,
        out_shape=(
            pltpu.VMEM(x.shape, BF16),
            pltpu.VMEM(spec_weights.shape, F32),
            pltpu.VMEM(x.shape, F32),
            pltpu.VMEM((1024, LANES), F32),
            pltpu.VMEM((64, 256), BF16),
        ),
        in_specs=[hbm] * 8,
        out_specs=(vmem,) * 5,
        scratch_shapes=[
            pltpu.VMEM((LANES, G * G), BF16),
            pltpu.VMEM((64, 64), BF16),
            pltpu.VMEM((1, 64), F32),
            pltpu.VMEM((2, 256, 256), BF16),
            pltpu.VMEM((2, J, 64, 256), BF16),
            pltpu.VMEM((4, 128, 128), BF16),
            pltpu.VMEM((2, 128, 128), BF16),
            pltpu.VMEM((M, J, 64, 128), BF16),
            pltpu.VMEM((LANES, G * G), BF16),
            pltpu.VMEM((LANES, G * G), BF16),
            pltpu.VMEM((4096, LANES), F32),
            pltpu.VMEM((NS * 16, LANES), F32),
            pltpu.VMEM((2 * J, ND * 16, LANES), F32),
            pltpu.VMEM((2 * J, ND * 16, LANES), F32),
            pltpu.VMEM((ND * 16, LANES), F32),
            pltpu.VMEM((4, J, NS, 16, LANES), BF16),
            pltpu.VMEM((4, J, NS, 16, LANES), BF16),
            pltpu.VMEM((4, 2 * J, ND, 16, LANES), BF16),
            pltpu.VMEM((4, 2 * J, ND, 16, LANES), BF16),
            pltpu.SemaphoreType.DMA((4, J)),
            pltpu.SemaphoreType.DMA((4, J)),
            pltpu.SemaphoreType.DMA((4, 2 * J)),
            pltpu.SemaphoreType.DMA((4, 2 * J)),
            pltpu.SemaphoreType.DMA((7,)),
            pltpu.SemaphoreType.DMA((4,)),
        ],
        compiler_params=pltpu.CompilerParams(
            collective_id=0, has_side_effects=True, vmem_limit_bytes=55 * 2**20
        ),
        cost_estimate=pl.CostEstimate(
            flops=2 * 10**9, bytes_accessed=12 * 2**20, transcendentals=2 * 10**6
        ),
    )(x, local_weight, bias.reshape(1, 64), zf_tables, zi_tables, jnp.asarray(small), spec_weights, cot)
    out, gin, gw = pl.pallas_call(
        finish,
        out_shape=(
            jax.ShapeDtypeStruct(x.shape, BF16),
            jax.ShapeDtypeStruct(x.shape, BF16),
            jax.ShapeDtypeStruct(spec_weights.shape, F32),
        ),
        in_specs=[vmem] * 5,
        out_specs=(hbm, hbm, hbm),
        scratch_shapes=[
            pltpu.VMEM(x.shape, BF16),
            pltpu.SemaphoreType.DMA((2,)),
            pltpu.SemaphoreType.DMA((4,)),
        ],
        compiler_params=pltpu.CompilerParams(vmem_limit_bytes=4 * 2**20),
    )(*parts)
    shape = fields.shape
    return out.reshape(shape), gin.reshape(shape), gw


def solution(mesh):
    placed = (
        P("dp", "space", None, None),
        P(None, ("dp", "space"), None, None),
        P(),
        P(),
        P("dp", "space", None, None),
    )
    return jax.shard_map(
        local,
        mesh=mesh,
        in_specs=placed,
        out_specs=(
            P("dp", "space", None, None),
            P("dp", "space", None, None),
            P(None, ("dp", "space"), None, None),
        ),
        check_vma=False,
    )
```

```python
import functools
import math

import jax
import jax.numpy as jnp
import ml_dtypes
import numpy as np
from jax import lax
from jax.experimental import pallas as pl
from jax.experimental.pallas import tpu as pltpu
from jax.sharding import PartitionSpec as P

MESH = pl.DeviceIdType.MESH
BF16 = jnp.bfloat16
F32 = jnp.float32

G = 64
M = 32
NS = 32
ND = 8
J = 4
LANES = 128
BLOCKS = 16

NT = (((1,), (1,)), ((), ()))
TN = (((0,), (0,)), ((), ()))


def tables():
    step = 2.0 * math.pi / G
    cell = np.arange(G)
    freq_z = np.arange(M)
    signed = np.where(np.arange(M) < M // 2, np.arange(M), G - M + np.arange(M))
    halves = np.where(freq_z == 0, 1.0, 2.0)
    angle = (freq_z[:, None] * cell[None, :] % G) * step
    z_rows = np.concatenate([np.cos(angle), -np.sin(angle)]) / 8
    z_rows_half = z_rows * np.tile(halves, 2)[:, None]
    four = np.eye(4)
    z_forward = np.kron(four, z_rows)
    z_forward_half = np.kron(four, z_rows_half)
    inv = np.stack([np.cos(angle), -np.sin(angle)], axis=1).reshape(2 * M, G) / 8
    inv_half = inv * np.repeat(halves, 2)[:, None]
    z_inverse, z_inverse_half = (
        np.kron(four, t).reshape(4, ND, J, 2, 256).transpose(2, 0, 1, 3, 4).reshape(J, 64, 256)
        for t in (inv, inv_half)
    )
    iy = np.arange(ND)[None, :] * 4 + np.arange(4)[:, None]
    ang_y = (signed[iy][:, :, None] * cell % G) * step
    c, s = np.cos(ang_y) / 8, np.sin(ang_y) / 8
    y_forward = np.stack([np.stack([c, s], -1), np.stack([-s, c], -1)], 1).reshape(64, 128)
    ct, st = c.transpose(2, 0, 1), s.transpose(2, 0, 1)
    y_inverse = np.stack([np.stack([ct, -st], 2), np.stack([st, ct], 2)], 0).reshape(128, 64)
    xs = 2 * np.arange(NS)[None, :] + np.arange(2)[:, None]
    ang_x = (signed[None, :, None] * xs[:, None, :] % G) * step
    c, s = np.cos(ang_x) / 8, np.sin(ang_x) / 8
    x_forward = np.stack([np.stack([c, s], 2), np.stack([-s, c], 2)], 1)
    x_forward = x_forward.reshape(128, 64)
    x_inverse = np.stack([c.transpose(0, 2, 1), s.transpose(0, 2, 1)]).reshape(128, M)
    return [
        t.astype(np.float32).astype(ml_dtypes.bfloat16)
        for t in (
            z_forward, z_forward_half, z_inverse, z_inverse_half,
            y_forward, y_inverse, x_forward, x_inverse,
        )
    ]


def dot(a, b, dims=(((1,), (0,)), ((), ()))):
    return lax.dot_general(a, b, dims, preferred_element_type=F32)


def farthest_first():
    def ring(i, n):
        return min(i, n - i)

    offsets = [(y, x, c) for y in range(4) for x in range(4) for c in range(2)][1:]
    offsets.sort(key=lambda o: -ring(o[0], 4) - ring(o[1], 4))
    return offsets, sorted(range(1, ND), key=lambda i: -ring(i, ND))


def kernel(
    x_hbm, weight_hbm, bias_hbm, zf_hbm, zi_hbm, small_hbm, w_hbm, cot_hbm,
    out_ref, gw_ref, acc_ref, a_ref, last_ref,
    x_ref, weight_ref, bias_ref, zf_ref, zi_ref, small_ref, mix_ref,
    w_ref, cot_ref, gp_ref,
    e_ref, f_ref, v_ref, u_ref, m_ref,
    send_s, recv_s, send_d, recv_d,
    sem_send_s, sem_recv_s, sem_send_d, sem_recv_d, sem_local, sem_x,
):
    d = lax.axis_index("dp")
    s = lax.axis_index("space")
    row_y, row_x, core = s // 8, lax.rem(s // 2, 4), lax.rem(s, 2)
    space_offsets, dp_offsets = farthest_first()

    def fetch(src, dst, sem):
        copy = pltpu.make_async_copy(src, dst, sem)
        copy.start()
        return copy

    quarter = G * G // 4
    zf_copy = fetch(zf_hbm, zf_ref, sem_local.at[0])
    x_copies = [
        fetch(
            x_hbm.at[:, pl.ds(i * quarter, quarter)],
            x_ref.at[:, pl.ds(i * quarter, quarter)],
            sem_x.at[i],
        )
        for i in range(4)
    ]
    small_copy = fetch(small_hbm, small_ref, sem_local.at[1])
    weight_copy = fetch(weight_hbm, weight_ref, sem_local.at[2])
    bias_copy = fetch(bias_hbm, bias_ref, sem_local.at[3])
    zi_copy = fetch(zi_hbm, zi_ref, sem_local.at[4])
    w_copy = fetch(w_hbm, w_ref, sem_local.at[5])
    cot_copy = fetch(cot_hbm, cot_ref, sem_local.at[6])

    barrier = pltpu.get_barrier_semaphore()

    def greet_space(i, carry):
        pl.semaphore_signal(barrier, inc=1, device_id=(d, lax.rem(s + i, NS)), device_id_type=MESH)
        return carry

    def greet_dp(i, carry):
        pl.semaphore_signal(barrier, inc=1, device_id=(lax.rem(d + i, ND), s), device_id_type=MESH)
        return carry

    lax.fori_loop(1, ND, greet_dp, 0)
    lax.fori_loop(1, NS, greet_space, 0)

    lo = lax.broadcasted_iota(jnp.int32, (1, LANES), 1) < 64
    sign = jnp.where(lo, 1.0, -1.0).astype(F32)

    def swap(v):
        return pltpu.roll(v, 64, 1)

    def exchange_space(n, c):
        src, dst = send_s.at[n, c], recv_s.at[n, c]
        for oy, ox, oc in space_offsets:
            t = lax.rem(row_y + oy, 4) * 8 + lax.rem(row_x + ox, 4) * 2 + lax.rem(core + oc, 2)
            pltpu.make_async_remote_copy(
                src_ref=src.at[t], dst_ref=dst.at[s],
                send_sem=sem_send_s.at[n, c], recv_sem=sem_recv_s.at[n, c],
                device_id=(d, t), device_id_type=MESH,
            ).start()
        pltpu.make_async_copy(src.at[s], dst.at[s], sem_recv_s.at[n, c]).start()

    def exchange_dp(n, g):
        src, dst = send_d.at[n, g], recv_d.at[n, g]
        for offset in dp_offsets:
            t = lax.rem(d + offset, ND)
            pltpu.make_async_remote_copy(
                src_ref=src.at[t], dst_ref=dst.at[d],
                send_sem=sem_send_d.at[n, g], recv_sem=sem_recv_d.at[n, g],
                device_id=(t, s), device_id_type=MESH,
            ).start()
        pltpu.make_async_copy(src.at[d], dst.at[d], sem_recv_d.at[n, g]).start()

    def arrived_space(n, c):
        pltpu.make_async_copy(recv_s.at[n, c], recv_s.at[n, c], sem_recv_s.at[n, c]).wait()

    def arrived_dp(n, g):
        pltpu.make_async_copy(recv_d.at[n, g], recv_d.at[n, g], sem_recv_d.at[n, g]).wait()

    def chunks(step, first=0, end=J):
        def go(c, carry):
            step(c)
            return carry

        lax.fori_loop(first, end, go, 0)

    def z_forward(block, table, q):
        e_ref[pl.ds(pl.multiple_of(q * 256, 256), 256), :] = dot(zf_ref[table], block, NT)

    def y_forward(n, c):
        table = small_ref[0, :64, :]
        for pair in range(4):
            parts = [
                e_ref[pl.ds((pair * 2 + e) * 4 + c, 128, stride=M), :].astype(BF16)
                for e in range(2)
            ]
            res = dot(table, jnp.concatenate(parts, axis=1)).astype(BF16)
            for e in range(2):
                for iyl in range(4):
                    send_s[n, c, iyl * 8 + pair * 2 + e] = res[
                        iyl * 16 : iyl * 16 + 16, e * 128 : e * 128 + 128
                    ]

    def x_forward(n_space, n_dp, c):
        f_ref[...] = recv_s[n_space, c].reshape(NS * 16, LANES).astype(F32)
        table = small_ref[2, :, :64]
        for pair in range(4):
            parts = []
            for e in range(2):
                row = pair * 2 + e
                parts.append(
                    jnp.concatenate(
                        [
                            f_ref[pl.ds(row, NS, stride=16), :],
                            f_ref[pl.ds(row + 8, NS, stride=16), :],
                        ],
                        axis=0,
                    ).astype(BF16)
                )
            res = dot(table, jnp.concatenate(parts, axis=1))
            for e in range(2):
                p00, p01, p10, p11 = (
                    res[b * 32 : b * 32 + 32, e * 128 : e * 128 + 128] for b in range(4)
                )
                both = jnp.where(lo, p00, p11) + swap(jnp.where(lo, p01, p10))
                both = both.astype(BF16)
                for h in range(2):
                    send_d[n_dp, c * 2 + h, pair * 2 + e] = both[h * 16 : h * 16 + 16]

    def widen_dp(n, g, to):
        to[g] = recv_d[n, g].reshape(ND * 16, LANES).astype(F32)

    def narrow_dp(n, g):
        send_d[n, g] = m_ref[...].astype(BF16).reshape(ND, 16, LANES)

    def x_inverse(n_dp, n_space, c):
        table = small_ref[3, :, :M]
        for pair in range(4):
            rhs = jnp.concatenate(
                [
                    jnp.concatenate(
                        [recv_d[n_dp, c * 2 + h, pair * 2 + e] for h in range(2)], axis=0
                    )
                    for e in range(2)
                ],
                axis=1,
            )
            res = dot(table, rhs)
            for e in range(2):
                c0, c1, s0, s1 = (
                    res[b * 32 : b * 32 + 32, e * 128 : e * 128 + 128] for b in range(4)
                )
                row = pair * 2 + e
                f_ref[pl.ds(row, NS, stride=16), :] = jnp.where(lo, c0, -s1) + swap(
                    jnp.where(lo, c1, -s0)
                )
                f_ref[pl.ds(row + 8, NS, stride=16), :] = jnp.where(lo, s0, c1) + swap(
                    jnp.where(lo, s1, c0)
                )
        send_s[n_space, c] = f_ref[...].astype(BF16).reshape(NS, 16, LANES)

    def y_inverse(n, c):
        table = small_ref[1, :, :64]
        for pair in range(4):
            parts = [
                jnp.concatenate(
                    [recv_s[n, c, iyl * 8 + pair * 2 + e] for iyl in range(4)], axis=0
                )
                for e in range(2)
            ]
            res = dot(table, jnp.concatenate(parts, axis=1))
            for e in range(2):
                izh = pair * 2 + e
                a_ref[izh * 128 : izh * 128 + 128, :] = res[:, e * 128 : e * 128 + 128]

    def cells(q):
        return pl.ds(pl.multiple_of(q * 256, 256), 256)

    zf_copy.wait()
    for i in range(4):
        x_copies[i].wait()
        for q in range(4 * i, 4 * i + 4):
            z_forward(x_ref[:, q * 256 : q * 256 + 256], 0, q)
    small_copy.wait()
    weight_copy.wait()
    bias_copy.wait()
    chunks(lambda c: y_forward(0, c))

    weight = weight_ref[...].astype(F32)
    zero = jnp.zeros((64, 64), F32)
    both = jnp.concatenate(
        [jnp.concatenate([weight, zero], axis=1), jnp.concatenate([zero, weight], axis=1)], axis=0
    )
    mix_ref[0] = both.T.astype(BF16)
    mix_ref[1] = both.astype(BF16)
    diagonal = lax.broadcasted_iota(jnp.int32, (64, 64), 0) == lax.broadcasted_iota(
        jnp.int32, (64, 64), 1
    )
    column = jnp.sum(jnp.where(diagonal, bias_ref[...], 0.0), axis=1, keepdims=True)
    bias = jnp.concatenate([column, column], axis=0)

    pl.semaphore_wait(barrier, NS + ND - 2)
    chunks(lambda c: exchange_space(0, c))

    def pointwise(q, carry):
        acc_ref[:, cells(q)] = dot(mix_ref[0], x_ref[:, cells(q)]) + bias
        return carry

    lax.fori_loop(0, BLOCKS, pointwise, 0, unroll=16)
    zi_copy.wait()
    last_ref[...] = zi_ref[0, J - 1]

    def out_dp(n):
        def step(c):
            arrived_space(n, c)
            x_forward(n, n, c)
            exchange_dp(n, c * 2)
            exchange_dp(n, c * 2 + 1)

        chunks(step)

    def back_space(n, c):
        arrived_dp(n, c * 2)
        arrived_dp(n, c * 2 + 1)
        x_inverse(n, n, c)
        exchange_space(n, c)

    def back_grid(n, table, c):
        arrived_space(n, c)
        y_inverse(n, c)

        def go(q, carry):
            acc_ref[:, cells(q)] += z_part(a_ref, zi_ref[table, c], q)
            return carry

        lax.fori_loop(0, BLOCKS, go, 0, unroll=16)

    out_dp(0)

    w_copy.wait()

    def twice(k, j):
        w = w_ref[k, j]
        return jnp.concatenate([w, w], axis=0)

    def mix(g):
        j, base = g // 2, lax.rem(g, 2) * 16
        arrived_dp(0, g)
        widen_dp(0, g, v_ref)

        def go(k, carry):
            rows = pl.ds(k, ND, stride=16)
            v = v_ref[g, rows, :]
            lhs = jnp.concatenate([jnp.where(lo, v, 0.0), jnp.where(lo, 0.0, v)], axis=0)
            res = dot(lhs.astype(BF16), twice(base + k, j))
            m_ref[rows, :] = res[:ND] - swap(res[ND:]) * sign
            return carry

        lax.fori_loop(0, 16, go, 0, unroll=16)
        narrow_dp(1, g)
        exchange_dp(1, g)

    chunks(mix, 0, 2 * J)
    chunks(lambda c: back_space(1, c))
    cot_copy.wait()
    chunks(lambda c: back_grid(1, 1, c), 0, J - 1)
    arrived_space(1, J - 1)
    y_inverse(1, J - 1)

    def middle(q, carry):
        pre = acc_ref[:, cells(q)] + z_part(a_ref, zi_ref[1, J - 1], q)
        cdf = 0.5 * (1.0 + lax.erf(pre * math.sqrt(0.5)))
        out_ref[:, cells(q)] = (pre * cdf).astype(BF16)
        pdf = jnp.exp(-0.5 * pre * pre) * (1.0 / math.sqrt(2.0 * math.pi))
        gp = (cot_ref[:, cells(q)].astype(F32) * (cdf + pre * pdf)).astype(BF16)
        gp_ref[:, cells(q)] = gp
        z_forward(gp, 1, q)
        return carry

    lax.fori_loop(0, BLOCKS, middle, 0, unroll=16)

    def out_space(c):
        y_forward(2, c)
        exchange_space(2, c)

    chunks(out_space)

    def pointwise_back(q, carry):
        acc_ref[:, cells(q)] = dot(mix_ref[1], gp_ref[:, cells(q)])
        return carry

    lax.fori_loop(0, BLOCKS, pointwise_back, 0, unroll=16)
    out_dp(2)

    def mix_grad(g):
        j, base = g // 2, lax.rem(g, 2) * 16
        arrived_dp(2, g)
        widen_dp(2, g, u_ref)

        def go(k, carry):
            rows = pl.ds(k, ND, stride=16)
            v = u_ref[g, rows, :]
            lhs = jnp.concatenate([v, swap(v) * sign], axis=0)
            res = dot(lhs.astype(BF16), twice(base + k, j), NT)
            m_ref[rows, :] = jnp.where(lo, res[:ND], res[ND:])
            return carry

        lax.fori_loop(0, 16, go, 0, unroll=16)
        narrow_dp(3, g)
        exchange_dp(3, g)

    chunks(mix_grad, 0, 2 * J)

    def weight_grad(g):
        j, base = g // 2, lax.rem(g, 2) * 16

        def go(k, carry):
            rows = pl.ds(k, ND, stride=16)
            v = v_ref[g, rows, :]
            grad = u_ref[g, rows, :]
            lhs = jnp.concatenate([v, swap(v)], axis=0).astype(BF16)
            rhs = jnp.concatenate([grad, swap(grad) * sign], axis=0).astype(BF16)
            gw_ref[base + k, j] = dot(lhs[:, :64], rhs, TN)
            return carry

        lax.fori_loop(0, 16, go, 0, unroll=16)

    def back_space_grad(c):
        back_space(3, c)
        weight_grad(c)

    chunks(back_space_grad, 0, 3)
    back_space(3, 3)

    def back_grid_grad(c):
        weight_grad(c * 2 + 3)
        back_grid(3, 0, c)
        weight_grad(c * 2 + 4)

    chunks(back_grid_grad, 0, 2)
    weight_grad(7)
    back_grid(3, 0, 2)
    arrived_space(3, J - 1)
    y_inverse(3, J - 1)

    for n in range(4):

        def sent_space(c, n=n):
            part = send_s.at[n, c, pl.ds(0, NS - 1)]
            pltpu.make_async_copy(part, part, sem_send_s.at[n, c]).wait()

        def sent_dp(g, n=n):
            part = send_d.at[n, g, pl.ds(0, ND - 1)]
            pltpu.make_async_copy(part, part, sem_send_d.at[n, g]).wait()

        chunks(sent_space)
        chunks(sent_dp, 0, 2 * J)


def z_part(a_ref, table, q):
    rows = [a_ref[pl.ds(q * 4 + yl, 16, stride=64), :] for yl in range(4)]
    return dot(jnp.concatenate(rows, axis=0).astype(BF16), table, TN)


def finish(
    out_ref, gw_ref, acc_ref, a_ref, last_ref,
    out_hbm, gin_hbm, gw_hbm,
    gin_ref, sem, sem_gin,
):
    copies = [
        pltpu.make_async_copy(gw_ref, gw_hbm, sem.at[0]),
        pltpu.make_async_copy(out_ref, out_hbm, sem.at[1]),
    ]
    for copy in copies:
        copy.start()
    quarter = G * G // 4
    for i in range(4):

        def last(q, carry):
            here = pl.ds(pl.multiple_of(q * 256, 256), 256)
            gin_ref[:, here] = (acc_ref[:, here] + z_part(a_ref, last_ref[...], q)).astype(BF16)
            return carry

        lax.fori_loop(4 * i, 4 * i + 4, last, 0, unroll=4)
        part = pl.ds(i * quarter, quarter)
        copy = pltpu.make_async_copy(gin_ref.at[:, part], gin_hbm.at[:, part], sem_gin.at[i])
        copy.start()
        copies.append(copy)
    for copy in copies:
        copy.wait()


def local(fields, spec_weights, local_weight, bias, cotangent):
    x = fields.reshape(LANES, G * G)
    cot = cotangent.reshape(LANES, G * G)
    made = tables()
    zf_tables = jnp.asarray(np.stack(made[0:2]))
    zi_tables = jnp.asarray(np.stack(made[2:4]))
    small = np.zeros((4, 128, 128), ml_dtypes.bfloat16)
    for i, t in enumerate(made[4:]):
        small[i, : t.shape[0], : t.shape[1]] = t
    hbm = pl.BlockSpec(memory_space=pltpu.HBM)
    vmem = pl.BlockSpec(memory_space=pltpu.VMEM)
    parts = pl.pallas_call(
        kernel,
        out_shape=(
            pltpu.VMEM(x.shape, BF16),
            pltpu.VMEM(spec_weights.shape, F32),
            pltpu.VMEM(x.shape, F32),
            pltpu.VMEM((1024, LANES), F32),
            pltpu.VMEM((64, 256), BF16),
        ),
        in_specs=[hbm] * 8,
        out_specs=(vmem,) * 5,
        scratch_shapes=[
            pltpu.VMEM((LANES, G * G), BF16),
            pltpu.VMEM((64, 64), BF16),
            pltpu.VMEM((1, 64), F32),
            pltpu.VMEM((2, 256, 256), BF16),
            pltpu.VMEM((2, J, 64, 256), BF16),
            pltpu.VMEM((4, 128, 128), BF16),
            pltpu.VMEM((2, 128, 128), BF16),
            pltpu.VMEM((M, J, 64, 128), BF16),
            pltpu.VMEM((LANES, G * G), BF16),
            pltpu.VMEM((LANES, G * G), BF16),
            pltpu.VMEM((4096, LANES), F32),
            pltpu.VMEM((NS * 16, LANES), F32),
            pltpu.VMEM((2 * J, ND * 16, LANES), F32),
            pltpu.VMEM((2 * J, ND * 16, LANES), F32),
            pltpu.VMEM((ND * 16, LANES), F32),
            pltpu.VMEM((4, J, NS, 16, LANES), BF16),
            pltpu.VMEM((4, J, NS, 16, LANES), BF16),
            pltpu.VMEM((4, 2 * J, ND, 16, LANES), BF16),
            pltpu.VMEM((4, 2 * J, ND, 16, LANES), BF16),
            pltpu.SemaphoreType.DMA((4, J)),
            pltpu.SemaphoreType.DMA((4, J)),
            pltpu.SemaphoreType.DMA((4, 2 * J)),
            pltpu.SemaphoreType.DMA((4, 2 * J)),
            pltpu.SemaphoreType.DMA((7,)),
            pltpu.SemaphoreType.DMA((4,)),
        ],
        compiler_params=pltpu.CompilerParams(
            collective_id=0, has_side_effects=True, vmem_limit_bytes=55 * 2**20
        ),
        cost_estimate=pl.CostEstimate(
            flops=2 * 10**9, bytes_accessed=12 * 2**20, transcendentals=2 * 10**6
        ),
    )(x, local_weight, bias.reshape(1, 64), zf_tables, zi_tables, jnp.asarray(small), spec_weights, cot)
    out, gin, gw = pl.pallas_call(
        finish,
        out_shape=(
            jax.ShapeDtypeStruct(x.shape, BF16),
            jax.ShapeDtypeStruct(x.shape, BF16),
            jax.ShapeDtypeStruct(spec_weights.shape, F32),
        ),
        in_specs=[vmem] * 5,
        out_specs=(hbm, hbm, hbm),
        scratch_shapes=[
            pltpu.VMEM(x.shape, BF16),
            pltpu.SemaphoreType.DMA((2,)),
            pltpu.SemaphoreType.DMA((4,)),
        ],
        compiler_params=pltpu.CompilerParams(vmem_limit_bytes=4 * 2**20),
    )(*parts)
    shape = fields.shape
    return out.reshape(shape), gin.reshape(shape), gw


def solution(mesh):
    placed = (
        P("dp", "space", None, None),
        P(None, ("dp", "space"), None, None),
        P(),
        P(),
        P("dp", "space", None, None),
    )
    return jax.shard_map(
        local,
        mesh=mesh,
        in_specs=placed,
        out_specs=(
            P("dp", "space", None, None),
            P("dp", "space", None, None),
            P(None, ("dp", "space"), None, None),
        ),
        check_vma=False,
    )
```

```python
import functools
import math

import jax
import jax.numpy as jnp
import ml_dtypes
import numpy as np
from jax import lax
from jax.experimental import pallas as pl
from jax.experimental.pallas import tpu as pltpu
from jax.sharding import PartitionSpec as P

MESH = pl.DeviceIdType.MESH
BF16 = jnp.bfloat16
F32 = jnp.float32

G = 64
M = 32
NS = 32
ND = 8
J = 4
LANES = 128
BLOCKS = 16

NT = (((1,), (1,)), ((), ()))
TN = (((0,), (0,)), ((), ()))


def tables():
    step = 2.0 * math.pi / G
    cell = np.arange(G)
    freq_z = np.arange(M)
    signed = np.where(np.arange(M) < M // 2, np.arange(M), G - M + np.arange(M))
    halves = np.where(freq_z == 0, 1.0, 2.0)
    angle = (freq_z[:, None] * cell[None, :] % G) * step
    z_rows = np.concatenate([np.cos(angle), -np.sin(angle)]) / 8
    z_rows_half = z_rows * np.tile(halves, 2)[:, None]
    four = np.eye(4)
    z_forward = np.kron(four, z_rows)
    z_forward_half = np.kron(four, z_rows_half)
    inv = np.stack([np.cos(angle), -np.sin(angle)], axis=1).reshape(2 * M, G) / 8
    inv_half = inv * np.repeat(halves, 2)[:, None]
    z_inverse, z_inverse_half = (
        np.kron(four, t).reshape(4, ND, J, 2, 256).transpose(2, 0, 1, 3, 4).reshape(J, 64, 256)
        for t in (inv, inv_half)
    )
    iy = np.arange(ND)[None, :] * 4 + np.arange(4)[:, None]
    ang_y = (signed[iy][:, :, None] * cell % G) * step
    c, s = np.cos(ang_y) / 8, np.sin(ang_y) / 8
    y_forward = np.stack([np.stack([c, s], -1), np.stack([-s, c], -1)], 1).reshape(64, 128)
    ct, st = c.transpose(2, 0, 1), s.transpose(2, 0, 1)
    y_inverse = np.stack([np.stack([ct, -st], 2), np.stack([st, ct], 2)], 0).reshape(128, 64)
    xs = 2 * np.arange(NS)[None, :] + np.arange(2)[:, None]
    ang_x = (signed[None, :, None] * xs[:, None, :] % G) * step
    c, s = np.cos(ang_x) / 8, np.sin(ang_x) / 8
    x_forward = np.stack([np.stack([c, s], 2), np.stack([-s, c], 2)], 1)
    x_forward = x_forward.reshape(128, 64)
    x_inverse = np.stack([c.transpose(0, 2, 1), s.transpose(0, 2, 1)]).reshape(128, M)
    return [
        t.astype(np.float32).astype(ml_dtypes.bfloat16)
        for t in (
            z_forward, z_forward_half, z_inverse, z_inverse_half,
            y_forward, y_inverse, x_forward, x_inverse,
        )
    ]


def dot(a, b, dims=(((1,), (0,)), ((), ()))):
    return lax.dot_general(a, b, dims, preferred_element_type=F32)


def farthest_first():
    def ring(i, n):
        return min(i, n - i)

    offsets = [(y, x, c) for y in range(4) for x in range(4) for c in range(2)][1:]
    offsets.sort(key=lambda o: -ring(o[0], 4) - ring(o[1], 4))
    return offsets, sorted(range(1, ND), key=lambda i: -ring(i, ND))


def kernel(
    x_hbm, weight_hbm, bias_hbm, zf_hbm, zi_hbm, small_hbm, w_hbm, cot_hbm,
    out_ref, gw_ref, acc_ref, a_ref, last_ref,
    x_ref, weight_ref, bias_ref, zf_ref, zi_ref, small_ref, mix_ref,
    w_ref, cot_ref, gp_ref,
    e_ref, f_ref, v_ref, u_ref, m_ref,
    send_s, recv_s, send_d, recv_d,
    sem_send_s, sem_recv_s, sem_send_d, sem_recv_d, sem_local, sem_x,
):
    d = lax.axis_index("dp")
    s = lax.axis_index("space")
    row_y, row_x, core = s // 8, lax.rem(s // 2, 4), lax.rem(s, 2)
    space_offsets, dp_offsets = farthest_first()

    def fetch(src, dst, sem):
        copy = pltpu.make_async_copy(src, dst, sem)
        copy.start()
        return copy

    barrier = pltpu.get_barrier_semaphore()

    def greet_space(i, carry):
        pl.semaphore_signal(barrier, inc=1, device_id=(d, lax.rem(s + i, NS)), device_id_type=MESH)
        return carry

    def greet_dp(i, carry):
        pl.semaphore_signal(barrier, inc=1, device_id=(lax.rem(d + i, ND), s), device_id_type=MESH)
        return carry

    lax.fori_loop(1, ND, greet_dp, 0)
    lax.fori_loop(1, NS, greet_space, 0)

    quarter = G * G // 4
    zf_copy = fetch(zf_hbm, zf_ref, sem_local.at[0])
    x_copies = [
        fetch(
            x_hbm.at[:, pl.ds(i * quarter, quarter)],
            x_ref.at[:, pl.ds(i * quarter, quarter)],
            sem_x.at[i],
        )
        for i in range(4)
    ]
    small_copy = fetch(small_hbm, small_ref, sem_local.at[1])
    weight_copy = fetch(weight_hbm, weight_ref, sem_local.at[2])
    bias_copy = fetch(bias_hbm, bias_ref, sem_local.at[3])
    zi_copy = fetch(zi_hbm, zi_ref, sem_local.at[4])
    w_copy = fetch(w_hbm, w_ref, sem_local.at[5])
    cot_copy = fetch(cot_hbm, cot_ref, sem_local.at[6])

    lo = lax.broadcasted_iota(jnp.int32, (1, LANES), 1) < 64
    sign = jnp.where(lo, 1.0, -1.0).astype(F32)

    def swap(v):
        return pltpu.roll(v, 64, 1)

    def exchange_space(n, c):
        src, dst = send_s.at[n, c], recv_s.at[n, c]
        for oy, ox, oc in space_offsets:
            t = lax.rem(row_y + oy, 4) * 8 + lax.rem(row_x + ox, 4) * 2 + lax.rem(core + oc, 2)
            pltpu.make_async_remote_copy(
                src_ref=src.at[t], dst_ref=dst.at[s],
                send_sem=sem_send_s.at[n, c], recv_sem=sem_recv_s.at[n, c],
                device_id=(d, t), device_id_type=MESH,
            ).start()
        pltpu.make_async_copy(src.at[s], dst.at[s], sem_recv_s.at[n, c]).start()

    def exchange_dp(n, g):
        src, dst = send_d.at[n, g], recv_d.at[n, g]
        for offset in dp_offsets:
            t = lax.rem(d + offset, ND)
            pltpu.make_async_remote_copy(
                src_ref=src.at[t], dst_ref=dst.at[d],
                send_sem=sem_send_d.at[n, g], recv_sem=sem_recv_d.at[n, g],
                device_id=(t, s), device_id_type=MESH,
            ).start()
        pltpu.make_async_copy(src.at[d], dst.at[d], sem_recv_d.at[n, g]).start()

    def arrived_space(n, c):
        pltpu.make_async_copy(recv_s.at[n, c], recv_s.at[n, c], sem_recv_s.at[n, c]).wait()

    def arrived_dp(n, g):
        pltpu.make_async_copy(recv_d.at[n, g], recv_d.at[n, g], sem_recv_d.at[n, g]).wait()

    def chunks(step, first=0, end=J):
        def go(c, carry):
            step(c)
            return carry

        lax.fori_loop(first, end, go, 0)

    def z_forward(block, table, q):
        e_ref[pl.ds(pl.multiple_of(q * 256, 256), 256), :] = dot(zf_ref[table], block, NT)

    def y_forward(n, c):
        table = small_ref[0, :64, :]
        for pair in range(4):
            parts = [
                e_ref[pl.ds((pair * 2 + e) * 4 + c, 128, stride=M), :].astype(BF16)
                for e in range(2)
            ]
            res = dot(table, jnp.concatenate(parts, axis=1)).astype(BF16)
            for e in range(2):
                for iyl in range(4):
                    send_s[n, c, iyl * 8 + pair * 2 + e] = res[
                        iyl * 16 : iyl * 16 + 16, e * 128 : e * 128 + 128
                    ]

    def x_forward(n_space, n_dp, c):
        f_ref[...] = recv_s[n_space, c].reshape(NS * 16, LANES).astype(F32)
        table = small_ref[2, :, :64]
        for pair in range(4):
            parts = []
            for e in range(2):
                row = pair * 2 + e
                parts.append(
                    jnp.concatenate(
                        [
                            f_ref[pl.ds(row, NS, stride=16), :],
                            f_ref[pl.ds(row + 8, NS, stride=16), :],
                        ],
                        axis=0,
                    ).astype(BF16)
                )
            res = dot(table, jnp.concatenate(parts, axis=1))
            for e in range(2):
                p00, p01, p10, p11 = (
                    res[b * 32 : b * 32 + 32, e * 128 : e * 128 + 128] for b in range(4)
                )
                both = jnp.where(lo, p00, p11) + swap(jnp.where(lo, p01, p10))
                send_d[n_dp, c, pair * 2 + e] = both.astype(BF16)

    def widen_dp(n, g, to):
        to[g] = recv_d[n, g].reshape(ND * M, LANES).astype(F32)

    def narrow_dp(n, g):
        send_d[n, g] = m_ref[...].astype(BF16).reshape(ND, M, LANES)

    def x_inverse(n_dp, n_space, c):
        table = small_ref[3, :, :M]
        for pair in range(4):
            rhs = jnp.concatenate(
                [recv_d[n_dp, c, pair * 2 + e] for e in range(2)], axis=1
            )
            res = dot(table, rhs)
            for e in range(2):
                c0, c1, s0, s1 = (
                    res[b * 32 : b * 32 + 32, e * 128 : e * 128 + 128] for b in range(4)
                )
                row = pair * 2 + e
                f_ref[pl.ds(row, NS, stride=16), :] = jnp.where(lo, c0, -s1) + swap(
                    jnp.where(lo, c1, -s0)
                )
                f_ref[pl.ds(row + 8, NS, stride=16), :] = jnp.where(lo, s0, c1) + swap(
                    jnp.where(lo, s1, c0)
                )
        send_s[n_space, c] = f_ref[...].astype(BF16).reshape(NS, 16, LANES)

    def y_inverse(n, c):
        table = small_ref[1, :, :64]
        for pair in range(4):
            parts = [
                jnp.concatenate(
                    [recv_s[n, c, iyl * 8 + pair * 2 + e] for iyl in range(4)], axis=0
                )
                for e in range(2)
            ]
            res = dot(table, jnp.concatenate(parts, axis=1))
            for e in range(2):
                izh = pair * 2 + e
                a_ref[izh * 128 : izh * 128 + 128, :] = res[:, e * 128 : e * 128 + 128]

    def cells(q):
        return pl.ds(pl.multiple_of(q * 256, 256), 256)

    zf_copy.wait()
    for i in range(4):
        x_copies[i].wait()
        for q in range(4 * i, 4 * i + 4):
            z_forward(x_ref[:, q * 256 : q * 256 + 256], 0, q)
    small_copy.wait()
    weight_copy.wait()
    bias_copy.wait()
    chunks(lambda c: y_forward(0, c))

    weight = weight_ref[...].astype(F32)
    zero = jnp.zeros((64, 64), F32)
    both = jnp.concatenate(
        [jnp.concatenate([weight, zero], axis=1), jnp.concatenate([zero, weight], axis=1)], axis=0
    )
    mix_ref[0] = both.T.astype(BF16)
    mix_ref[1] = both.astype(BF16)
    diagonal = lax.broadcasted_iota(jnp.int32, (64, 64), 0) == lax.broadcasted_iota(
        jnp.int32, (64, 64), 1
    )
    column = jnp.sum(jnp.where(diagonal, bias_ref[...], 0.0), axis=1, keepdims=True)
    bias = jnp.concatenate([column, column], axis=0)

    pl.semaphore_wait(barrier, NS + ND - 2)
    chunks(lambda c: exchange_space(0, c))

    def pointwise(q, carry):
        acc_ref[:, cells(q)] = dot(mix_ref[0], x_ref[:, cells(q)]) + bias
        return carry

    lax.fori_loop(0, BLOCKS, pointwise, 0, unroll=16)
    zi_copy.wait()
    last_ref[...] = zi_ref[0, J - 1]

    def out_dp(n):
        def step(c):
            arrived_space(n, c)
            x_forward(n, n, c)
            exchange_dp(n, c)

        chunks(step)

    def back_space(n, c):
        arrived_dp(n, c)
        x_inverse(n, n, c)
        exchange_space(n, c)

    def back_grid(n, table, c):
        arrived_space(n, c)
        y_inverse(n, c)

        def go(q, carry):
            acc_ref[:, cells(q)] += z_part(a_ref, zi_ref[table, c], q)
            return carry

        lax.fori_loop(0, BLOCKS, go, 0, unroll=16)

    out_dp(0)

    w_copy.wait()

    def twice(k, j):
        w = w_ref[k, j]
        return jnp.concatenate([w, w], axis=0)

    def mix(g):
        arrived_dp(0, g)
        widen_dp(0, g, v_ref)

        def go(k, carry):
            rows = pl.ds(k, ND, stride=M)
            v = v_ref[g, rows, :]
            lhs = jnp.concatenate([jnp.where(lo, v, 0.0), jnp.where(lo, 0.0, v)], axis=0)
            res = dot(lhs.astype(BF16), twice(k, g))
            m_ref[rows, :] = res[:ND] - swap(res[ND:]) * sign
            return carry

        lax.fori_loop(0, M, go, 0, unroll=16)
        narrow_dp(1, g)
        exchange_dp(1, g)

    chunks(mix)
    chunks(lambda c: back_space(1, c))
    cot_copy.wait()
    chunks(lambda c: back_grid(1, 1, c), 0, J - 1)
    arrived_space(1, J - 1)
    y_inverse(1, J - 1)

    def middle(pair, carry):
        sums = z_part_pair(a_ref, zi_ref[1, J - 1], pair)
        grads = []
        for e in range(2):
            q = pair * 2 + e
            pre = acc_ref[:, cells(q)] + sums[e * 128 : e * 128 + 128]
            cdf = 0.5 * (1.0 + lax.erf(pre * math.sqrt(0.5)))
            out_ref[:, cells(q)] = (pre * cdf).astype(BF16)
            pdf = jnp.exp(-0.5 * pre * pre) * (1.0 / math.sqrt(2.0 * math.pi))
            gp = (cot_ref[:, cells(q)].astype(F32) * (cdf + pre * pdf)).astype(BF16)
            gp_ref[:, cells(q)] = gp
            grads.append(gp)
        res = dot(zf_ref[1], jnp.concatenate(grads, axis=0), NT)
        for e in range(2):
            e_ref[cells(pair * 2 + e), :] = res[:, e * 128 : e * 128 + 128]
        return carry

    lax.fori_loop(0, BLOCKS // 2, middle, 0, unroll=BLOCKS // 2)

    def out_space(c):
        y_forward(2, c)
        exchange_space(2, c)

    chunks(out_space)

    def pointwise_back(q, carry):
        acc_ref[:, cells(q)] = dot(mix_ref[1], gp_ref[:, cells(q)])
        return carry

    lax.fori_loop(0, BLOCKS, pointwise_back, 0, unroll=16)
    out_dp(2)

    def mix_grad(g):
        arrived_dp(2, g)
        widen_dp(2, g, u_ref)

        def go(k, carry):
            rows = pl.ds(k, ND, stride=M)
            v = u_ref[g, rows, :]
            lhs = jnp.concatenate([v, swap(v) * sign], axis=0)
            res = dot(lhs.astype(BF16), twice(k, g), NT)
            m_ref[rows, :] = jnp.where(lo, res[:ND], res[ND:])
            return carry

        lax.fori_loop(0, M, go, 0, unroll=16)
        narrow_dp(3, g)
        exchange_dp(3, g)

    chunks(mix_grad)

    def weight_grad(g):

        def go(k, carry):
            rows = pl.ds(k, ND, stride=M)
            v = v_ref[g, rows, :]
            grad = u_ref[g, rows, :]
            lhs = jnp.concatenate([v, swap(v)], axis=0).astype(BF16)
            rhs = jnp.concatenate([grad, swap(grad) * sign], axis=0).astype(BF16)
            gw_ref[k, g] = dot(lhs[:, :64], rhs, TN)
            return carry

        lax.fori_loop(0, M, go, 0, unroll=16)

    def back_space_grad(c):
        back_space(3, c)
        weight_grad(c)

    chunks(back_space_grad)
    chunks(lambda c: back_grid(3, 0, c), 0, J - 1)
    arrived_space(3, J - 1)
    y_inverse(3, J - 1)

    for n in range(4):

        def sent_space(c, n=n):
            part = send_s.at[n, c, pl.ds(0, NS - 1)]
            pltpu.make_async_copy(part, part, sem_send_s.at[n, c]).wait()

        def sent_dp(g, n=n):
            part = send_d.at[n, g, pl.ds(0, ND - 1)]
            pltpu.make_async_copy(part, part, sem_send_d.at[n, g]).wait()

        chunks(sent_space)
        chunks(sent_dp)


def z_part(a_ref, table, q):
    rows = [a_ref[pl.ds(q * 4 + yl, 16, stride=64), :] for yl in range(4)]
    return dot(jnp.concatenate(rows, axis=0).astype(BF16), table, TN)


def z_part_pair(a_ref, table, pair):
    blocks = [
        jnp.concatenate(
            [a_ref[pl.ds((pair * 2 + e) * 4 + yl, 16, stride=64), :] for yl in range(4)], axis=0
        ).astype(BF16)
        for e in range(2)
    ]
    return dot(jnp.concatenate(blocks, axis=1), table, TN)


def finish(
    out_ref, gw_ref, acc_ref, a_ref, last_ref,
    out_hbm, gin_hbm, gw_hbm,
    gin_ref, sem, sem_gin,
):
    copies = [
        pltpu.make_async_copy(gw_ref, gw_hbm, sem.at[0]),
        pltpu.make_async_copy(out_ref, out_hbm, sem.at[1]),
    ]
    for copy in copies:
        copy.start()
    quarter = G * G // 4
    for i in range(4):

        def last(q, carry):
            here = pl.ds(pl.multiple_of(q * 256, 256), 256)
            gin_ref[:, here] = (acc_ref[:, here] + z_part(a_ref, last_ref[...], q)).astype(BF16)
            return carry

        lax.fori_loop(4 * i, 4 * i + 4, last, 0, unroll=4)
        part = pl.ds(i * quarter, quarter)
        copy = pltpu.make_async_copy(gin_ref.at[:, part], gin_hbm.at[:, part], sem_gin.at[i])
        copy.start()
        copies.append(copy)
    for copy in copies:
        copy.wait()


def local(fields, spec_weights, local_weight, bias, cotangent):
    x = fields.reshape(LANES, G * G)
    cot = cotangent.reshape(LANES, G * G)
    made = tables()
    zf_tables = jnp.asarray(np.stack(made[0:2]))
    zi_tables = jnp.asarray(np.stack(made[2:4]))
    small = np.zeros((4, 128, 128), ml_dtypes.bfloat16)
    for i, t in enumerate(made[4:]):
        small[i, : t.shape[0], : t.shape[1]] = t
    hbm = pl.BlockSpec(memory_space=pltpu.HBM)
    vmem = pl.BlockSpec(memory_space=pltpu.VMEM)
    parts = pl.pallas_call(
        kernel,
        out_shape=(
            pltpu.VMEM(x.shape, BF16),
            pltpu.VMEM(spec_weights.shape, F32),
            pltpu.VMEM(x.shape, F32),
            pltpu.VMEM((1024, LANES), F32),
            pltpu.VMEM((64, 256), BF16),
        ),
        in_specs=[hbm] * 8,
        out_specs=(vmem,) * 5,
        scratch_shapes=[
            pltpu.VMEM((LANES, G * G), BF16),
            pltpu.VMEM((64, 64), BF16),
            pltpu.VMEM((1, 64), F32),
            pltpu.VMEM((2, 256, 256), BF16),
            pltpu.VMEM((2, J, 64, 256), BF16),
            pltpu.VMEM((4, 128, 128), BF16),
            pltpu.VMEM((2, 128, 128), BF16),
            pltpu.VMEM((M, J, 64, 128), BF16),
            pltpu.VMEM((LANES, G * G), BF16),
            pltpu.VMEM((LANES, G * G), BF16),
            pltpu.VMEM((4096, LANES), F32),
            pltpu.VMEM((NS * 16, LANES), F32),
            pltpu.VMEM((J, ND * M, LANES), F32),
            pltpu.VMEM((J, ND * M, LANES), F32),
            pltpu.VMEM((ND * M, LANES), F32),
            pltpu.VMEM((4, J, NS, 16, LANES), BF16),
            pltpu.VMEM((4, J, NS, 16, LANES), BF16),
            pltpu.VMEM((4, J, ND, M, LANES), BF16),
            pltpu.VMEM((4, J, ND, M, LANES), BF16),
            pltpu.SemaphoreType.DMA((4, J)),
            pltpu.SemaphoreType.DMA((4, J)),
            pltpu.SemaphoreType.DMA((4, J)),
            pltpu.SemaphoreType.DMA((4, J)),
            pltpu.SemaphoreType.DMA((7,)),
            pltpu.SemaphoreType.DMA((4,)),
        ],
        compiler_params=pltpu.CompilerParams(
            collective_id=0, has_side_effects=True, vmem_limit_bytes=55 * 2**20
        ),
        cost_estimate=pl.CostEstimate(
            flops=2 * 10**9, bytes_accessed=12 * 2**20, transcendentals=2 * 10**6
        ),
    )(x, local_weight, bias.reshape(1, 64), zf_tables, zi_tables, jnp.asarray(small), spec_weights, cot)
    out, gin, gw = pl.pallas_call(
        finish,
        out_shape=(
            jax.ShapeDtypeStruct(x.shape, BF16),
            jax.ShapeDtypeStruct(x.shape, BF16),
            jax.ShapeDtypeStruct(spec_weights.shape, F32),
        ),
        in_specs=[vmem] * 5,
        out_specs=(hbm, hbm, hbm),
        scratch_shapes=[
            pltpu.VMEM(x.shape, BF16),
            pltpu.SemaphoreType.DMA((2,)),
            pltpu.SemaphoreType.DMA((4,)),
        ],
        compiler_params=pltpu.CompilerParams(vmem_limit_bytes=4 * 2**20),
    )(*parts)
    shape = fields.shape
    return out.reshape(shape), gin.reshape(shape), gw


def solution(mesh):
    placed = (
        P("dp", "space", None, None),
        P(None, ("dp", "space"), None, None),
        P(),
        P(),
        P("dp", "space", None, None),
    )
    return jax.shard_map(
        local,
        mesh=mesh,
        in_specs=placed,
        out_specs=(
            P("dp", "space", None, None),
            P("dp", "space", None, None),
            P(None, ("dp", "space"), None, None),
        ),
        check_vma=False,
    )
```

```python
import functools
import math

import jax
import jax.numpy as jnp
import ml_dtypes
import numpy as np
from jax import lax
from jax.experimental import pallas as pl
from jax.experimental.pallas import tpu as pltpu
from jax.sharding import PartitionSpec as P

MESH = pl.DeviceIdType.MESH
BF16 = jnp.bfloat16
F32 = jnp.float32

G = 64
M = 32
NS = 32
ND = 8
J = 4
LANES = 128
BLOCKS = 16

NT = (((1,), (1,)), ((), ()))
TN = (((0,), (0,)), ((), ()))


def tables():
    step = 2.0 * math.pi / G
    cell = np.arange(G)
    freq_z = np.arange(M)
    signed = np.where(np.arange(M) < M // 2, np.arange(M), G - M + np.arange(M))
    halves = np.where(freq_z == 0, 1.0, 2.0)
    angle = (freq_z[:, None] * cell[None, :] % G) * step
    z_rows = np.concatenate([np.cos(angle), -np.sin(angle)]) / 8
    z_rows_half = z_rows * np.tile(halves, 2)[:, None]
    four = np.eye(4)
    z_forward = np.kron(four, z_rows)
    z_forward_half = np.kron(four, z_rows_half)
    inv = np.stack([np.cos(angle), -np.sin(angle)], axis=1).reshape(2 * M, G) / 8
    inv_half = inv * np.repeat(halves, 2)[:, None]
    z_inverse, z_inverse_half = (
        np.kron(four, t).reshape(4, ND, J, 2, 256).transpose(2, 0, 1, 3, 4).reshape(J, 64, 256)
        for t in (inv, inv_half)
    )
    iy = np.arange(ND)[None, :] * 4 + np.arange(4)[:, None]
    ang_y = (signed[iy][:, :, None] * cell % G) * step
    c, s = np.cos(ang_y) / 8, np.sin(ang_y) / 8
    y_forward = np.stack([np.stack([c, s], -1), np.stack([-s, c], -1)], 1).reshape(64, 128)
    ct, st = c.transpose(2, 0, 1), s.transpose(2, 0, 1)
    y_inverse = np.stack([np.stack([ct, -st], 2), np.stack([st, ct], 2)], 0).reshape(128, 64)
    xs = 2 * np.arange(NS)[None, :] + np.arange(2)[:, None]
    ang_x = (signed[None, :, None] * xs[:, None, :] % G) * step
    c, s = np.cos(ang_x) / 8, np.sin(ang_x) / 8
    x_forward = np.stack([np.stack([c, s], 2), np.stack([-s, c], 2)], 1)
    x_forward = x_forward.reshape(128, 64)
    x_inverse = np.stack([c.transpose(0, 2, 1), s.transpose(0, 2, 1)]).reshape(128, M)
    return [
        t.astype(np.float32).astype(ml_dtypes.bfloat16)
        for t in (
            z_forward, z_forward_half, z_inverse, z_inverse_half,
            y_forward, y_inverse, x_forward, x_inverse,
        )
    ]


def dot(a, b, dims=(((1,), (0,)), ((), ()))):
    return lax.dot_general(a, b, dims, preferred_element_type=F32)


def farthest_first():
    def ring(i, n):
        return min(i, n - i)

    offsets = [(y, x, c) for y in range(4) for x in range(4) for c in range(2)][1:]
    offsets.sort(key=lambda o: -ring(o[0], 4) - ring(o[1], 4))
    return offsets, sorted(range(1, ND), key=lambda i: -ring(i, ND))


def kernel(
    x_hbm, weight_hbm, bias_hbm, zf_hbm, zi_hbm, small_hbm, w_hbm, cot_hbm,
    out_ref, gw_ref, acc_ref, a_ref, last_ref,
    x_ref, weight_ref, bias_ref, zf_ref, zi_ref, small_ref, mix_ref,
    w_ref, cot_ref, gp_ref,
    e_ref, f_ref, v_ref, u_ref, m_ref,
    send_s, recv_s, send_d, recv_d,
    sem_send_s, sem_recv_s, sem_send_d, sem_recv_d, sem_local, sem_x,
):
    d = lax.axis_index("dp")
    s = lax.axis_index("space")
    row_y, row_x, core = s // 8, lax.rem(s // 2, 4), lax.rem(s, 2)
    space_offsets, dp_offsets = farthest_first()

    def fetch(src, dst, sem):
        copy = pltpu.make_async_copy(src, dst, sem)
        copy.start()
        return copy

    barrier = pltpu.get_barrier_semaphore()

    def greet_space(i, carry):
        pl.semaphore_signal(barrier, inc=1, device_id=(d, lax.rem(s + i, NS)), device_id_type=MESH)
        return carry

    def greet_dp(i, carry):
        pl.semaphore_signal(barrier, inc=1, device_id=(lax.rem(d + i, ND), s), device_id_type=MESH)
        return carry

    lax.fori_loop(1, ND, greet_dp, 0)
    lax.fori_loop(1, NS, greet_space, 0)

    quarter = G * G // 4
    zf_copy = fetch(zf_hbm, zf_ref, sem_local.at[0])
    x_copies = [
        fetch(
            x_hbm.at[:, pl.ds(i * quarter, quarter)],
            x_ref.at[:, pl.ds(i * quarter, quarter)],
            sem_x.at[i],
        )
        for i in range(4)
    ]
    small_copy = fetch(small_hbm, small_ref, sem_local.at[1])
    weight_copy = fetch(weight_hbm, weight_ref, sem_local.at[2])
    bias_copy = fetch(bias_hbm, bias_ref, sem_local.at[3])
    zi_copy = fetch(zi_hbm, zi_ref, sem_local.at[4])
    w_copy = fetch(w_hbm, w_ref, sem_local.at[5])
    cot_copy = fetch(cot_hbm, cot_ref, sem_local.at[6])

    lo = lax.broadcasted_iota(jnp.int32, (1, LANES), 1) < 64
    sign = jnp.where(lo, 1.0, -1.0).astype(F32)

    def swap(v):
        return pltpu.roll(v, 64, 1)

    def exchange_space(n, c):
        src, dst = send_s.at[n, c], recv_s.at[n, c]
        for oy, ox, oc in space_offsets:
            t = lax.rem(row_y + oy, 4) * 8 + lax.rem(row_x + ox, 4) * 2 + lax.rem(core + oc, 2)
            pltpu.make_async_remote_copy(
                src_ref=src.at[t], dst_ref=dst.at[s],
                send_sem=sem_send_s.at[n, c], recv_sem=sem_recv_s.at[n, c],
                device_id=(d, t), device_id_type=MESH,
            ).start()
        pltpu.make_async_copy(src.at[s], dst.at[s], sem_recv_s.at[n, c]).start()

    def exchange_dp(n, g):
        src, dst = send_d.at[n, g], recv_d.at[n, g]
        for offset in dp_offsets:
            t = lax.rem(d + offset, ND)
            pltpu.make_async_remote_copy(
                src_ref=src.at[t], dst_ref=dst.at[d],
                send_sem=sem_send_d.at[n, g], recv_sem=sem_recv_d.at[n, g],
                device_id=(t, s), device_id_type=MESH,
            ).start()
        pltpu.make_async_copy(src.at[d], dst.at[d], sem_recv_d.at[n, g]).start()

    def arrived_space(n, c):
        pltpu.make_async_copy(recv_s.at[n, c], recv_s.at[n, c], sem_recv_s.at[n, c]).wait()

    def arrived_dp(n, g):
        pltpu.make_async_copy(recv_d.at[n, g], recv_d.at[n, g], sem_recv_d.at[n, g]).wait()

    def chunks(step, first=0, end=J):
        def go(c, carry):
            step(c)
            return carry

        lax.fori_loop(first, end, go, 0)

    def z_forward(block, table, q):
        e_ref[pl.ds(pl.multiple_of(q * 256, 256), 256), :] = dot(zf_ref[table], block, NT)

    def y_forward(n, c):
        parts = [e_ref[pl.ds(izh * 4 + c, 128, stride=M), :].astype(BF16) for izh in range(8)]
        res = dot(small_ref[0, :64, :], jnp.concatenate(parts, axis=1)).astype(BF16)
        for izh in range(8):
            for iyl in range(4):
                send_s[n, c, iyl * 8 + izh] = res[
                    iyl * 16 : iyl * 16 + 16, izh * 128 : izh * 128 + 128
                ]

    def x_forward(n_space, n_dp, c):
        f_ref[...] = recv_s[n_space, c].reshape(NS * 16, LANES).astype(F32)
        table = small_ref[2, :, :64]
        for pair in range(4):
            parts = []
            for e in range(2):
                row = pair * 2 + e
                parts.append(
                    jnp.concatenate(
                        [
                            f_ref[pl.ds(row, NS, stride=16), :],
                            f_ref[pl.ds(row + 8, NS, stride=16), :],
                        ],
                        axis=0,
                    ).astype(BF16)
                )
            res = dot(table, jnp.concatenate(parts, axis=1))
            for e in range(2):
                p00, p01, p10, p11 = (
                    res[b * 32 : b * 32 + 32, e * 128 : e * 128 + 128] for b in range(4)
                )
                both = jnp.where(lo, p00, p11) + swap(jnp.where(lo, p01, p10))
                send_d[n_dp, c, pair * 2 + e] = both.astype(BF16)

    def widen_dp(n, g, to):
        to[g] = recv_d[n, g].reshape(ND * M, LANES).astype(F32)

    def narrow_dp(n, g):
        send_d[n, g] = m_ref[...].astype(BF16).reshape(ND, M, LANES)

    def x_inverse(n_dp, n_space, c):
        table = small_ref[3, :, :M]
        for pair in range(4):
            rhs = jnp.concatenate(
                [recv_d[n_dp, c, pair * 2 + e] for e in range(2)], axis=1
            )
            res = dot(table, rhs)
            for e in range(2):
                c0, c1, s0, s1 = (
                    res[b * 32 : b * 32 + 32, e * 128 : e * 128 + 128] for b in range(4)
                )
                row = pair * 2 + e
                f_ref[pl.ds(row, NS, stride=16), :] = jnp.where(lo, c0, -s1) + swap(
                    jnp.where(lo, c1, -s0)
                )
                f_ref[pl.ds(row + 8, NS, stride=16), :] = jnp.where(lo, s0, c1) + swap(
                    jnp.where(lo, s1, c0)
                )
        send_s[n_space, c] = f_ref[...].astype(BF16).reshape(NS, 16, LANES)

    def y_inverse(n, c):
        table = small_ref[1, :, :64]
        for pair in range(4):
            parts = [
                jnp.concatenate(
                    [recv_s[n, c, iyl * 8 + pair * 2 + e] for iyl in range(4)], axis=0
                )
                for e in range(2)
            ]
            res = dot(table, jnp.concatenate(parts, axis=1))
            for e in range(2):
                izh = pair * 2 + e
                a_ref[izh * 128 : izh * 128 + 128, :] = res[:, e * 128 : e * 128 + 128]

    def cells(q):
        return pl.ds(pl.multiple_of(q * 256, 256), 256)

    zf_copy.wait()
    for i in range(4):
        x_copies[i].wait()
        for q in range(4 * i, 4 * i + 4):
            z_forward(x_ref[:, q * 256 : q * 256 + 256], 0, q)
    small_copy.wait()
    weight_copy.wait()
    bias_copy.wait()
    chunks(lambda c: y_forward(0, c))

    weight = weight_ref[...].astype(F32)
    zero = jnp.zeros((64, 64), F32)
    both = jnp.concatenate(
        [jnp.concatenate([weight, zero], axis=1), jnp.concatenate([zero, weight], axis=1)], axis=0
    )
    mix_ref[0] = both.T.astype(BF16)
    mix_ref[1] = both.astype(BF16)
    diagonal = lax.broadcasted_iota(jnp.int32, (64, 64), 0) == lax.broadcasted_iota(
        jnp.int32, (64, 64), 1
    )
    column = jnp.sum(jnp.where(diagonal, bias_ref[...], 0.0), axis=1, keepdims=True)
    bias = jnp.concatenate([column, column], axis=0)

    pl.semaphore_wait(barrier, NS + ND - 2)
    chunks(lambda c: exchange_space(0, c))

    def pointwise(q, carry):
        acc_ref[:, cells(q)] = dot(mix_ref[0], x_ref[:, cells(q)]) + bias
        return carry

    lax.fori_loop(0, BLOCKS, pointwise, 0, unroll=16)
    zi_copy.wait()
    last_ref[...] = zi_ref[0, J - 1]

    def out_dp(n):
        def step(c):
            arrived_space(n, c)
            x_forward(n, n, c)
            exchange_dp(n, c)

        chunks(step)

    def back_space(n, c):
        arrived_dp(n, c)
        x_inverse(n, n, c)
        exchange_space(n, c)

    def back_grid(n, table, c):
        arrived_space(n, c)
        y_inverse(n, c)

        def go(q, carry):
            acc_ref[:, cells(q)] += z_part(a_ref, zi_ref[table, c], q)
            return carry

        lax.fori_loop(0, BLOCKS, go, 0, unroll=16)

    out_dp(0)

    w_copy.wait()

    def twice(k, j):
        w = w_ref[k, j]
        return jnp.concatenate([w, w], axis=0)

    def mix(g):
        arrived_dp(0, g)
        widen_dp(0, g, v_ref)

        def go(k, carry):
            rows = pl.ds(k, ND, stride=M)
            v = v_ref[g, rows, :]
            lhs = jnp.concatenate([jnp.where(lo, v, 0.0), jnp.where(lo, 0.0, v)], axis=0)
            res = dot(lhs.astype(BF16), twice(k, g))
            m_ref[rows, :] = res[:ND] - swap(res[ND:]) * sign
            return carry

        lax.fori_loop(0, M, go, 0, unroll=32)
        narrow_dp(1, g)
        exchange_dp(1, g)

    chunks(mix)
    chunks(lambda c: back_space(1, c))
    cot_copy.wait()
    chunks(lambda c: back_grid(1, 1, c), 0, J - 1)
    arrived_space(1, J - 1)
    y_inverse(1, J - 1)

    def middle(pair, carry):
        sums = z_part_pair(a_ref, zi_ref[1, J - 1], pair)
        grads = []
        for e in range(2):
            q = pair * 2 + e
            pre = acc_ref[:, cells(q)] + sums[e * 128 : e * 128 + 128]
            cdf = 0.5 * (1.0 + lax.erf(pre * math.sqrt(0.5)))
            out_ref[:, cells(q)] = (pre * cdf).astype(BF16)
            pdf = jnp.exp(-0.5 * pre * pre) * (1.0 / math.sqrt(2.0 * math.pi))
            gp = (cot_ref[:, cells(q)].astype(F32) * (cdf + pre * pdf)).astype(BF16)
            gp_ref[:, cells(q)] = gp
            grads.append(gp)
        res = dot(zf_ref[1], jnp.concatenate(grads, axis=0), NT)
        for e in range(2):
            e_ref[cells(pair * 2 + e), :] = res[:, e * 128 : e * 128 + 128]
        return carry

    lax.fori_loop(0, BLOCKS // 2, middle, 0, unroll=BLOCKS // 2)

    def out_space(c):
        y_forward(2, c)
        exchange_space(2, c)

    chunks(out_space)

    def pointwise_back(q, carry):
        acc_ref[:, cells(q)] = dot(mix_ref[1], gp_ref[:, cells(q)])
        return carry

    lax.fori_loop(0, BLOCKS, pointwise_back, 0, unroll=16)
    out_dp(2)

    def mix_grad(g):
        arrived_dp(2, g)
        widen_dp(2, g, u_ref)

        def go(k, carry):
            rows = pl.ds(k, ND, stride=M)
            v = u_ref[g, rows, :]
            lhs = jnp.concatenate([v, swap(v) * sign], axis=0)
            res = dot(lhs.astype(BF16), twice(k, g), NT)
            m_ref[rows, :] = jnp.where(lo, res[:ND], res[ND:])
            return carry

        lax.fori_loop(0, M, go, 0, unroll=32)
        narrow_dp(3, g)
        exchange_dp(3, g)

    chunks(mix_grad)

    def weight_grad(g):

        def go(k, carry):
            rows = pl.ds(k, ND, stride=M)
            v = v_ref[g, rows, :]
            grad = u_ref[g, rows, :]
            lhs = jnp.concatenate([v, swap(v)], axis=0).astype(BF16)
            rhs = jnp.concatenate([grad, swap(grad) * sign], axis=0).astype(BF16)
            gw_ref[k, g] = dot(lhs[:, :64], rhs, TN)
            return carry

        lax.fori_loop(0, M, go, 0, unroll=16)

    def back_space_grad(c):
        back_space(3, c)
        weight_grad(c)

    chunks(back_space_grad)
    chunks(lambda c: back_grid(3, 0, c), 0, J - 1)
    arrived_space(3, J - 1)
    y_inverse(3, J - 1)

    for n in range(4):

        def sent_space(c, n=n):
            part = send_s.at[n, c, pl.ds(0, NS - 1)]
            pltpu.make_async_copy(part, part, sem_send_s.at[n, c]).wait()

        def sent_dp(g, n=n):
            part = send_d.at[n, g, pl.ds(0, ND - 1)]
            pltpu.make_async_copy(part, part, sem_send_d.at[n, g]).wait()

        chunks(sent_space)
        chunks(sent_dp)


def z_part(a_ref, table, q):
    rows = [a_ref[pl.ds(q * 4 + yl, 16, stride=64), :] for yl in range(4)]
    return dot(jnp.concatenate(rows, axis=0).astype(BF16), table, TN)


def z_part_pair(a_ref, table, pair):
    blocks = [
        jnp.concatenate(
            [a_ref[pl.ds((pair * 2 + e) * 4 + yl, 16, stride=64), :] for yl in range(4)], axis=0
        ).astype(BF16)
        for e in range(2)
    ]
    return dot(jnp.concatenate(blocks, axis=1), table, TN)


def finish(
    out_ref, gw_ref, acc_ref, a_ref, last_ref,
    out_hbm, gin_hbm, gw_hbm,
    gin_ref, sem, sem_gin,
):
    copies = [
        pltpu.make_async_copy(gw_ref, gw_hbm, sem.at[0]),
        pltpu.make_async_copy(out_ref, out_hbm, sem.at[1]),
    ]
    for copy in copies:
        copy.start()
    quarter = G * G // 4
    for i in range(4):
        for pair in range(2 * i, 2 * i + 2):
            sums = z_part_pair(a_ref, last_ref[...], pair)
            for e in range(2):
                here = pl.ds((pair * 2 + e) * 256, 256)
                gin_ref[:, here] = (
                    acc_ref[:, here] + sums[e * 128 : e * 128 + 128]
                ).astype(BF16)
        part = pl.ds(i * quarter, quarter)
        copy = pltpu.make_async_copy(gin_ref.at[:, part], gin_hbm.at[:, part], sem_gin.at[i])
        copy.start()
        copies.append(copy)
    for copy in copies:
        copy.wait()


def local(fields, spec_weights, local_weight, bias, cotangent):
    x = fields.reshape(LANES, G * G)
    cot = cotangent.reshape(LANES, G * G)
    made = tables()
    zf_tables = jnp.asarray(np.stack(made[0:2]))
    zi_tables = jnp.asarray(np.stack(made[2:4]))
    small = np.zeros((4, 128, 128), ml_dtypes.bfloat16)
    for i, t in enumerate(made[4:]):
        small[i, : t.shape[0], : t.shape[1]] = t
    hbm = pl.BlockSpec(memory_space=pltpu.HBM)
    vmem = pl.BlockSpec(memory_space=pltpu.VMEM)
    parts = pl.pallas_call(
        kernel,
        out_shape=(
            pltpu.VMEM(x.shape, BF16),
            pltpu.VMEM(spec_weights.shape, F32),
            pltpu.VMEM(x.shape, F32),
            pltpu.VMEM((1024, LANES), F32),
            pltpu.VMEM((64, 256), BF16),
        ),
        in_specs=[hbm] * 8,
        out_specs=(vmem,) * 5,
        scratch_shapes=[
            pltpu.VMEM((LANES, G * G), BF16),
            pltpu.VMEM((64, 64), BF16),
            pltpu.VMEM((1, 64), F32),
            pltpu.VMEM((2, 256, 256), BF16),
            pltpu.VMEM((2, J, 64, 256), BF16),
            pltpu.VMEM((4, 128, 128), BF16),
            pltpu.VMEM((2, 128, 128), BF16),
            pltpu.VMEM((M, J, 64, 128), BF16),
            pltpu.VMEM((LANES, G * G), BF16),
            pltpu.VMEM((LANES, G * G), BF16),
            pltpu.VMEM((4096, LANES), F32),
            pltpu.VMEM((NS * 16, LANES), F32),
            pltpu.VMEM((J, ND * M, LANES), F32),
            pltpu.VMEM((J, ND * M, LANES), F32),
            pltpu.VMEM((ND * M, LANES), F32),
            pltpu.VMEM((4, J, NS, 16, LANES), BF16),
            pltpu.VMEM((4, J, NS, 16, LANES), BF16),
            pltpu.VMEM((4, J, ND, M, LANES), BF16),
            pltpu.VMEM((4, J, ND, M, LANES), BF16),
            pltpu.SemaphoreType.DMA((4, J)),
            pltpu.SemaphoreType.DMA((4, J)),
            pltpu.SemaphoreType.DMA((4, J)),
            pltpu.SemaphoreType.DMA((4, J)),
            pltpu.SemaphoreType.DMA((7,)),
            pltpu.SemaphoreType.DMA((4,)),
        ],
        compiler_params=pltpu.CompilerParams(
            collective_id=0, has_side_effects=True, vmem_limit_bytes=55 * 2**20
        ),
        cost_estimate=pl.CostEstimate(
            flops=2 * 10**9, bytes_accessed=12 * 2**20, transcendentals=2 * 10**6
        ),
    )(x, local_weight, bias.reshape(1, 64), zf_tables, zi_tables, jnp.asarray(small), spec_weights, cot)
    out, gin, gw = pl.pallas_call(
        finish,
        out_shape=(
            jax.ShapeDtypeStruct(x.shape, BF16),
            jax.ShapeDtypeStruct(x.shape, BF16),
            jax.ShapeDtypeStruct(spec_weights.shape, F32),
        ),
        in_specs=[vmem] * 5,
        out_specs=(hbm, hbm, hbm),
        scratch_shapes=[
            pltpu.VMEM(x.shape, BF16),
            pltpu.SemaphoreType.DMA((2,)),
            pltpu.SemaphoreType.DMA((4,)),
        ],
        compiler_params=pltpu.CompilerParams(vmem_limit_bytes=4 * 2**20),
    )(*parts)
    shape = fields.shape
    return out.reshape(shape), gin.reshape(shape), gw


def solution(mesh):
    placed = (
        P("dp", "space", None, None),
        P(None, ("dp", "space"), None, None),
        P(),
        P(),
        P("dp", "space", None, None),
    )
    return jax.shard_map(
        local,
        mesh=mesh,
        in_specs=placed,
        out_specs=(
            P("dp", "space", None, None),
            P("dp", "space", None, None),
            P(None, ("dp", "space"), None, None),
        ),
        check_vma=False,
    )
```
